768 devices in a mesh: dp: 48 (over x, z), feat: 16 (over y, core).
Axes of the slice: x: 4, y: 8, z: 12, core: 2. Of those that a mesh axis runs over, the one named last changes fastest.
Arguments:
- activations: bfloat16 [12288, 8192], P('dp', 'feat'), may hold values from -6 to 6
- cotangent: bfloat16 [12288, 1024], P('dp'), may hold values from -0.053955078 to 0.053955078
- weight: float32 [8192, 1024], P('feat'), may hold values from -0.0625 to 0.0625
- stats_old: float32 [16, 48, 2, 256, 256], P('feat', 'dp'), as said below
- owners: int32 [32, 4], replicated, may hold values from 0 to 47, as said below
- next_acts: bfloat16 [12288, 8192], P('dp', 'feat'), may hold values from -6 to 6
Outputs:
- weight_new: float32 [8192, 1024], P('feat')
- stats_new: float32 [16, 48, 2, 256, 256], P('feat', 'dp')
- next_out: bfloat16 [12288, 1024], P('dp', 'feat')
The draws below stay inside these ranges and needn't reach their ends.
Inputs may be any that keep to these rules, and one draw needn't show every extreme that they name: `owners`: blocks are grouped by the index of feat that holds their rows (8192 / (256 * 16) row blocks a group); in every group each dp index owns at most 2 blocks, and some dp index owns exactly 2. `stats_old`: every slot holds a symmetric positive definite matrix; slots that no block maps to are not read.
All inputs are finite; a program needn't handle non-finite values.
Results may differ from the reference program's by a relative error of at most 0.02.
Values may be sent and summed in bfloat16 or wider, within the bound.
No kernel may reach another device: no remote copies, remote signals or barrier semaphores. Data moves between devices by JAX's collectives and lax.ppermute only.
A program may use at most 128 MiB of HBM per device.

```python
import jax
import jax.numpy as jnp
from jax import lax

D = 8192
COLS = 1024
BLOCK = 256
ITERS = 6
TOKENS = 12288
MOST = 2
N_DP = 48
N_FEAT = 16


def draw_owners(key, part):
    block_count = D // (BLOCK * N_FEAT) * (COLS // BLOCK)
    group_keys = jax.random.split(jax.random.fold_in(key, 11), N_FEAT)
    order_keys = jax.random.split(jax.random.fold_in(key, 23), N_FEAT)
    chosen = jax.vmap(lambda sub: jax.random.permutation(sub, N_DP))(group_keys).astype(jnp.int32)
    place_ids = jnp.arange(block_count, dtype=jnp.int32)
    pick_ids = jnp.where(place_ids < MOST, 0, 1 + jnp.maximum(place_ids - MOST, 0) % (N_DP - 1)).astype(jnp.int32)
    listing = chosen[:, pick_ids]
    shuffle = jax.vmap(lambda sub: jax.random.permutation(sub, block_count))(order_keys).astype(jnp.int32)
    placed = jnp.take_along_axis(listing, shuffle, axis=1)
    return placed.reshape(D // BLOCK, COLS // BLOCK).astype(jnp.int32)


def draw_stats_old(key, part):
    shape = (N_FEAT, N_DP, MOST, BLOCK, BLOCK)
    base = jax.random.normal(jax.random.fold_in(key, 31), shape, jnp.float32)
    product = jnp.einsum('abcij,abckj->abcik', base, base, precision=lax.Precision.HIGHEST) / BLOCK
    identity = jnp.eye(BLOCK, dtype=jnp.float32)
    return (product + 0.125 * identity).astype(jnp.float32)


def block_scale(key, dims, shards, smallest, high):
    factor_of = 1.0
    for dim, blocks in shards:
        draws = jax.random.uniform(jax.random.fold_in(jax.random.fold_in(key, 6), dim), (blocks,), jnp.float32, smallest / len(shards), high / len(shards))
        factor_of = factor_of * jnp.repeat(jnp.exp(draws), dims[dim] // blocks).reshape((-1,) + (1,) * (len(dims) - 1 - dim))
    return factor_of


def noise(own_key, dims, spread, limit, cuts=(), kind=jnp.bfloat16):
    result = spread * jax.random.normal(own_key, dims, jnp.float32)
    if cuts:
        result = result * block_scale(own_key, dims, cuts, -0.22, 0.18)
    return jnp.clip(result, -limit, limit).astype(kind)


def setup_inputs(seed: int = 0) -> dict:
    key_list = jax.random.split(jax.random.key(seed), 7)
    return {
        "activations": noise(key_list[0], (TOKENS, D), 1.0, 6.0, ((0, 48), (1, 16))),
        "cotangent": noise(key_list[1], (TOKENS, COLS), (TOKENS ** -0.5), 0.053955078, ((0, 48),)),
        "weight": noise(key_list[2], (D, COLS), D ** -0.5, 0.0625, ((0, 16),), jnp.float32),
        "stats_old": draw_stats_old(jax.random.fold_in(key_list[6], 71), 0),
        "owners": draw_owners(jax.random.fold_in(key_list[6], 71), 0),
        "next_acts": noise(key_list[5], (TOKENS, D), 1.0, 6.0, ((0, 48), (1, 16))),
    }


decay_rate = 0.9
step_rate = 0.01

def newton_root(stats):
    width = stats.shape[0]
    identity = jnp.eye(width, dtype=jnp.float32)
    norm_value = jnp.sqrt(jnp.sum(stats * stats) + 1e-06)
    matrix = stats / norm_value
    iterate = identity
    for counter in range(ITERS):
        factor = (5.0 * identity - matrix) / 4.0
        factor_low = factor.astype(jnp.bfloat16)
        iterate = jnp.dot(iterate.astype(jnp.bfloat16), factor_low, preferred_element_type=jnp.float32)
        if counter + 1 < ITERS:
            square = jnp.dot(factor_low, factor_low, preferred_element_type=jnp.float32).astype(jnp.bfloat16)
            fourth = jnp.dot(square, square, preferred_element_type=jnp.float32).astype(jnp.bfloat16)
            matrix = jnp.dot(fourth, matrix.astype(jnp.bfloat16), preferred_element_type=jnp.float32)
    return iterate * norm_value ** (-0.25)

def one_block(pair):
    grad_block, old_stats = pair
    gram = jnp.dot(grad_block, grad_block.T, preferred_element_type=jnp.float32) / BLOCK
    renewed = decay_rate * old_stats + (1.0 - decay_rate) * gram
    root_matrix = newton_root(renewed)
    update = jnp.dot(root_matrix.astype(jnp.bfloat16), grad_block, preferred_element_type=jnp.float32)
    return (renewed, update)

def reference(activations, cotangent, weight, stats_old, owners, next_acts):
    grad = jnp.dot(activations.T, cotangent, preferred_element_type=jnp.float32)
    grad_low = grad.astype(jnp.bfloat16)
    row_count = D // BLOCK
    col_blocks = COLS // BLOCK
    block_count = D // (BLOCK * N_FEAT) * col_blocks
    blocks = grad_low.reshape(row_count, BLOCK, col_blocks, BLOCK).transpose(0, 2, 1, 3).reshape(row_count * col_blocks, BLOCK, BLOCK)
    own_list = owners.reshape(-1).astype(jnp.int32)
    block_ids = jnp.arange(row_count * col_blocks, dtype=jnp.int32)
    group_id = block_ids // block_count
    same_owner = (own_list[:, None] == own_list[None, :]) & (group_id[:, None] == group_id[None, :]) & (block_ids[None, :] < block_ids[:, None])
    slot_of = lax.optimization_barrier(jnp.sum(same_owner.astype(jnp.int32), axis=1)).astype(jnp.int32)
    old_stats = stats_old[group_id, own_list, slot_of]
    renewed_all, update_all = lax.map(one_block, (blocks, old_stats))
    update = update_all.reshape(row_count, col_blocks, BLOCK, BLOCK).transpose(0, 2, 1, 3).reshape(D, COLS)
    weight_new = weight - step_rate * update
    stats_new = jnp.zeros(stats_old.shape, jnp.float32).at[group_id, own_list, slot_of].set(renewed_all)
    next_out = jnp.dot(next_acts, weight_new.astype(jnp.bfloat16), preferred_element_type=jnp.float32).astype(jnp.bfloat16)
    return (weight_new, stats_new, next_out)
```

```python
import functools

import jax
import jax.numpy as jnp
from jax import lax
from jax.experimental import pallas as pl
from jax.experimental.pallas import tpu as pltpu
from jax.sharding import Mesh
from jax.sharding import PartitionSpec as P

ITERS = 6
DP = ("x", "z")
BF = jnp.bfloat16
F32 = jnp.float32
decay_rate = 0.9
step_rate = 0.01

W = 256
H = W // 2
SENT = 2 * W + 2 * H + 32
VMEM = pltpu.CompilerParams(vmem_limit_bytes=48 * 1024 * 1024)


def place(rows):
    return pl.BlockSpec(memory_space=rows)


IN_VMEM = place(pltpu.VMEM)
IN_SMEM = place(pltpu.SMEM)


def dims(rows, cols):
    return (
        lax.broadcasted_iota(jnp.int32, (rows, cols), 0),
        lax.broadcasted_iota(jnp.int32, (rows, cols), 1),
    )


def mine_and_slot(owners, where, block, cols):
    me, base = where[0], where[1]
    slot = jnp.int32(0)
    for before in range(block):
        slot += (owners[base + before // cols, before % cols] == me).astype(jnp.int32)
    return owners[base + block // cols, block % cols] == me, slot


def grad_kernel(where, owners, acts, cot, stats, out):
    cols = out.shape[0]
    row, col = dims(H, H)
    for i in range(cols):
        out[i, : 2 * W, :] = lax.dot_general(
            acts[...], cot[:, i * W : (i + 1) * W], (((0,), (0,)), ((), ())), preferred_element_type=F32
        ).astype(BF)
        out[i, 2 * W :, :] = jnp.zeros((SENT - 2 * W, W), BF)
        for r in range(2):
            mine, slot = mine_and_slot(owners, where, r * cols + i, cols)

            @pl.when(mine)
            def _(i=i, r=r, slot=slot):
                old = stats[0, 0, jnp.minimum(slot, stats.shape[2] - 1)]
                upper, lower = old[:H, :H], old[H:, H:]
                start = 2 * W + r * H
                out[i, start : start + H, :H] = old[:H, H:].astype(BF)
                out[i, start : start + H, H:] = jnp.where(col >= row, upper, lower).astype(BF)
                diagonal = jnp.sum(jnp.where(row == col, lower, 0.0), axis=0, keepdims=True)
                start = 2 * W + 2 * H + r * 16
                out[i, start : start + 16, :H] = jnp.broadcast_to(diagonal, (16, H)).astype(BF)


def sum_x_kernel(tiles, out):
    total = tiles[0].astype(F32)
    for i in range(1, tiles.shape[0]):
        total += tiles[i].astype(F32)
    out[: total.shape[0], :] = total.astype(BF)
    rest = out.shape[0] - total.shape[0]
    if rest:
        out[total.shape[0] :, :] = jnp.zeros((rest, W), BF)


def sum_z_kernel(tiles, out):
    total = tiles[0].astype(F32)
    for i in range(1, tiles.shape[0]):
        total += tiles[i].astype(F32)
    total = total.astype(BF)
    for i in range(out.shape[0]):
        out[i] = total


def dot(a, b):
    return jnp.dot(a, b, preferred_element_type=F32)


def root_kernel(tile, out):
    row, col = dims(H, H)
    big_row, big_col = dims(W, W)
    identity = (big_row == big_col).astype(F32)
    grads, matrices, iterates, norms = [], [], [], []
    for r in range(2):
        grad = tile[r * W : (r + 1) * W, :]
        packed = tile[2 * W + r * H : 2 * W + (r + 1) * H, :].astype(F32)
        diagonal = tile[2 * W + 2 * H + r * 16 : 2 * W + 2 * H + (r + 1) * 16, :H][:1, :].astype(F32)
        flipped = packed.T
        both, both_t = packed[:, H:], flipped[H:, :]
        upper = jnp.where(col >= row, both, both_t)
        lower = jnp.where(col < row, both, jnp.where(col > row, both_t, jnp.broadcast_to(diagonal, (H, H))))
        old = jnp.concatenate(
            [
                jnp.concatenate([upper, packed[:, :H]], axis=1),
                jnp.concatenate([flipped[:H, :], lower], axis=1),
            ],
            axis=0,
        )
        gram = lax.dot_general(grad, grad, (((1,), (1,)), ((), ())), preferred_element_type=F32) / W
        renewed = decay_rate * old + (1.0 - decay_rate) * gram
        norm = jnp.sqrt(jnp.sum(renewed * renewed, axis=(0, 1), keepdims=True) + 1e-06)
        grads.append(grad)
        matrices.append(renewed / norm)
        norms.append(norm)
        iterates.append(None)
    for step in range(ITERS):
        for r in range(2):
            low = ((5.0 * identity - matrices[r]) / 4.0).astype(BF)
            if step == 0:
                iterates[r] = low.astype(F32)
            else:
                iterates[r] = dot(iterates[r].astype(BF), low)
            if step + 1 < ITERS:
                square = dot(low, low).astype(BF)
                fourth = dot(square, square).astype(BF)
                matrices[r] = dot(fourth, matrices[r].astype(BF))
    for r in range(2):
        scale = lax.rsqrt(jnp.sqrt(norms[r]))
        root = (iterates[r] * scale).astype(BF)
        update = dot(root, grads[r]).astype(BF)
        for i in range(out.shape[0]):
            out[i, r * W : (r + 1) * W, :] = update


def next_kernel(weight, update, acts, weight_new, out):
    new = weight[...] - step_rate * update[0].astype(F32)
    weight_new[...] = new
    out[...] = lax.dot_general(
        new.astype(BF), acts[...], (((0,), (1,)), ((), ())), preferred_element_type=F32
    ).astype(BF)


def stats_kernel(where, owners, grads, stats, out):
    cols = grads.shape[0]
    out[...] = jnp.zeros(out.shape, F32)
    for i in range(cols):
        for r in range(2):
            mine, slot = mine_and_slot(owners, where, r * cols + i, cols)

            @pl.when(mine)
            def _(i=i, r=r, slot=slot):
                at = jnp.minimum(slot, stats.shape[2] - 1)
                grad = grads[i, r * W : (r + 1) * W, :]
                gram = lax.dot_general(grad, grad, (((1,), (1,)), ((), ())), preferred_element_type=F32) / W
                out[0, 0, at] = decay_rate * stats[0, 0, at] + (1.0 - decay_rate) * gram


def call(kernel, out, *args, specs=None):
    return pl.pallas_call(
        kernel,
        out_shape=out,
        in_specs=specs or [IN_VMEM] * len(args),
        out_specs=jax.tree.map(lambda _: IN_VMEM, out),
        compiler_params=VMEM,
    )(*args)


def swap(x, axis):
    return lax.all_to_all(x, axis, 0, 0, tiled=True)


def body(activations, cotangent, weight, stats_old, owners, next_acts):
    n_x, n_z, n_feat = (lax.axis_size(a) for a in ("x", "z", "feat"))
    rows_dev, columns = weight.shape
    tokens = activations.shape[0]
    share = -(-SENT // (8 * n_z)) * 8
    where = jnp.stack([lax.axis_index("x") * n_z + lax.axis_index("z"), lax.axis_index("feat") * (rows_dev // W)])
    shape = jax.ShapeDtypeStruct
    sent = call(
        grad_kernel,
        shape((n_x, SENT, W), BF),
        where,
        owners,
        activations,
        cotangent,
        stats_old,
        specs=[IN_SMEM, IN_SMEM, IN_VMEM, IN_VMEM, IN_VMEM],
    )
    column = call(sum_x_kernel, shape((n_z * share, W), BF), swap(sent, "x"))
    mine = call(sum_z_kernel, shape((n_z, share, W), BF), swap(column.reshape(n_z, share, W), "z"))
    full = swap(mine, "z").reshape(n_z * share, W)
    grads = lax.all_gather(full[: 2 * W], "x", axis=0, tiled=False)
    updates = swap(call(root_kernel, shape((n_x, 2 * W, W), BF), full), "x")
    weight_new, partial_next = pl.pallas_call(
        next_kernel,
        grid=(n_x,),
        in_specs=[
            pl.BlockSpec((rows_dev, W), lambda i: (0, i)),
            pl.BlockSpec((1, rows_dev, W), lambda i: (i, 0, 0)),
            pl.BlockSpec((tokens, rows_dev), lambda i: (0, 0)),
        ],
        out_specs=[
            pl.BlockSpec((rows_dev, W), lambda i: (0, i)),
            pl.BlockSpec((W, tokens), lambda i: (i, 0)),
        ],
        out_shape=[shape((rows_dev, columns), F32), shape((columns, tokens), BF)],
        compiler_params=VMEM,
    )(weight, updates, next_acts)
    tiles = swap(partial_next.reshape(n_feat, columns // n_feat, tokens), "feat")
    next_out = jnp.sum(tiles.astype(F32), axis=0).astype(BF).T
    stats_new = call(
        stats_kernel,
        shape(stats_old.shape, F32),
        where,
        owners,
        grads,
        stats_old,
        specs=[IN_SMEM, IN_SMEM, IN_VMEM, IN_VMEM],
    )
    return (weight_new, stats_new, next_out)


def solution(mesh):
    torus = Mesh(mesh.devices.reshape(4, 12, mesh.shape["feat"]), ("x", "z", "feat"))
    return jax.shard_map(
        body,
        mesh=torus,
        in_specs=(
            P(DP, "feat"),
            P(DP, None),
            P("feat", None),
            P("feat", DP, None, None, None),
            P(),
            P(DP, "feat"),
        ),
        out_specs=(P("feat", None), P("feat", DP, None, None, None), P(DP, "feat")),
        check_vma=False,
    )
```

```python
import jax
import jax.numpy as jnp
from jax import lax
from jax.experimental import pallas as pl
from jax.experimental.pallas import tpu as pltpu
from jax.sharding import Mesh
from jax.sharding import PartitionSpec as P

ITERS = 6
DP = ("x", "zh", "zl")
BF = jnp.bfloat16
F32 = jnp.float32
decay_rate = 0.9
step_rate = 0.01

W = 256
H = W // 2
SENT = 2 * W + 2 * H + 32


def room(mib):
    return pltpu.CompilerParams(vmem_limit_bytes=mib * 1024 * 1024)


IN_VMEM = pl.BlockSpec(memory_space=pltpu.VMEM)
IN_SMEM = pl.BlockSpec(memory_space=pltpu.SMEM)


def dims(rows, cols):
    return (
        lax.broadcasted_iota(jnp.int32, (rows, cols), 0),
        lax.broadcasted_iota(jnp.int32, (rows, cols), 1),
    )


def mine_and_slot(owners, where, block, cols, count):
    me, base = where[0], where[1]
    mine = jnp.int32(0)
    slot = jnp.int32(0)
    for other in range(count):
        held = (owners[other % cols, base + other // cols] == me).astype(jnp.int32)
        slot += jnp.where(other < block, held, 0)
        mine += jnp.where(other == block, held, 0)
    return mine == 1, slot


def grad_kernel(where, owners, acts, cot, stats, out, turned):
    cols = pl.num_programs(0)
    i = pl.program_id(0)
    row, col = dims(H, H)

    @pl.when(i == 0)
    def _():
        turned[...] = acts[...].T

    out[0, : 2 * W, :] = jnp.dot(turned[...], cot[...], preferred_element_type=F32).astype(BF)
    out[0, 2 * W :, :] = jnp.zeros((SENT - 2 * W, W), BF)
    for r in range(2):
        mine, slot = mine_and_slot(owners, where, r * 4 + i, 4, 8)

        @pl.when(mine)
        def _(r=r, slot=slot):
            old = stats[0, 0, jnp.minimum(slot, stats.shape[2] - 1)]
            upper, lower = old[:H, :H], old[H:, H:]
            start = 2 * W + r * H
            out[0, start : start + H, :H] = old[:H, H:].astype(BF)
            out[0, start : start + H, H:] = jnp.where(col >= row, upper, lower).astype(BF)
            diagonal = jnp.sum(jnp.where(row == col, lower, 0.0), axis=0, keepdims=True)
            start = 2 * W + 2 * H + r * 16
            out[0, start : start + 16, :H] = jnp.broadcast_to(diagonal, (16, H)).astype(BF)


def sum_kernel(tiles, out):
    total = tiles[0].astype(F32)
    for i in range(1, tiles.shape[0]):
        total += tiles[i].astype(F32)
    total = total.astype(BF)
    for i in range(out.shape[0]):
        out[i] = total


def dot(a, b):
    return jnp.dot(a, b, preferred_element_type=F32)


def root_kernel(where, tile, weight, own, first, second, third, sent, out):
    row, col = dims(H, H)
    big_row, big_col = dims(W, W)
    identity = (big_row == big_col).astype(F32)
    grads, matrices, iterates, norms = [], [], [], []
    for r in range(2):
        grad = tile[r * W : (r + 1) * W, :]
        packed = tile[2 * W + r * H : 2 * W + (r + 1) * H, :].astype(F32)
        diagonal = tile[2 * W + 2 * H + r * 16 : 2 * W + 2 * H + (r + 1) * 16, :H][:1, :].astype(F32)
        flipped = packed.T
        both, both_t = packed[:, H:], flipped[H:, :]
        upper = jnp.where(col >= row, both, both_t)
        lower = jnp.where(col < row, both, jnp.where(col > row, both_t, jnp.broadcast_to(diagonal, (H, H))))
        old = jnp.concatenate(
            [
                jnp.concatenate([upper, packed[:, :H]], axis=1),
                jnp.concatenate([flipped[:H, :], lower], axis=1),
            ],
            axis=0,
        )
        gram = lax.dot_general(grad, grad, (((1,), (1,)), ((), ())), preferred_element_type=F32) / W
        renewed = decay_rate * old + (1.0 - decay_rate) * gram
        norm = jnp.sqrt(jnp.sum(renewed * renewed, axis=(0, 1), keepdims=True) + 1e-06)
        grads.append(grad)
        matrices.append(renewed / norm)
        norms.append(norm)
        iterates.append(None)
        sent[(2 + r) * W : (3 + r) * W, :] = grad
    for step in range(ITERS):
        for r in range(2):
            low = ((5.0 * identity - matrices[r]) / 4.0).astype(BF)
            if step == 0:
                iterates[r] = low.astype(F32)
            else:
                iterates[r] = dot(iterates[r].astype(BF), low)
            if step + 1 < ITERS:
                square = dot(low, low).astype(BF)
                fourth = dot(square, square).astype(BF)
                matrices[r] = dot(fourth, matrices[r].astype(BF))
    news = []
    for r in range(2):
        root = (iterates[r] * lax.rsqrt(jnp.sqrt(norms[r]))).astype(BF)
        update = dot(root, grads[r]).astype(BF)
        sent[r * W : (r + 1) * W, :] = update
        news.append((weight[r * W : (r + 1) * W, :] - step_rate * update.astype(F32)).astype(BF))
    new = jnp.concatenate(news, axis=0)
    for k, acts in enumerate((own, first, second, third)):
        part = lax.dot_general(new, acts[...], (((0,), (1,)), ((), ())), preferred_element_type=F32).astype(BF)
        plane = (where[2] + (4 - k)) % 4
        out[pl.ds(pl.multiple_of(plane * W, W), W), :] = part


def finish_kernel(where, owners, own, first, second, third, weight, stats, weight_new, stats_new):
    stats_new[...] = jnp.zeros(stats_new.shape, F32)
    for k, part in enumerate((own, first, second, third)):
        column = (where[2] + (4 - k)) % 4
        at = pl.ds(pl.multiple_of(column * W, W), W)
        weight_new[:, at] = weight[:, at] - step_rate * part[: 2 * W, :].astype(F32)
        for r in range(2):
            mine, slot = mine_and_slot(owners, where, r * 4 + column, 4, 8)

            @pl.when(mine)
            def _(r=r, slot=slot, part=part):
                place = jnp.minimum(slot, stats.shape[2] - 1)
                grad = part[(2 + r) * W : (3 + r) * W, :]
                gram = lax.dot_general(grad, grad, (((1,), (1,)), ((), ())), preferred_element_type=F32) / W
                stats_new[0, 0, place] = decay_rate * stats[0, 0, place] + (1.0 - decay_rate) * gram


def call(kernel, out, *args, specs=None):
    return pl.pallas_call(
        kernel,
        out_shape=out,
        in_specs=specs or [IN_VMEM] * len(args),
        out_specs=jax.tree.map(lambda _: IN_VMEM, out),
        compiler_params=room(32),
    )(*args)


def swap(x, axis):
    return lax.all_to_all(x, axis, 0, 0, tiled=True)


def turn(x, axis, by):
    n = lax.axis_size(axis)
    return lax.ppermute(x, axis, [(i, (i + by) % n) for i in range(n)])


def body(activations, cotangent, weight, stats_old, owners, next_acts):
    n_x, n_zh, n_zl, n_feat = (lax.axis_size(a) for a in ("x", "zh", "zl", "feat"))
    rows_dev, columns = weight.shape
    tokens = activations.shape[0]
    x_index = lax.axis_index("x")
    where = jnp.stack(
        [
            (x_index * n_zh + lax.axis_index("zh")) * n_zl + lax.axis_index("zl"),
            lax.axis_index("feat") * (rows_dev // W),
            x_index,
        ]
    )
    owners = owners.T
    shape = jax.ShapeDtypeStruct
    sent = pl.pallas_call(
        grad_kernel,
        grid_spec=pltpu.PrefetchScalarGridSpec(
            num_scalar_prefetch=2,
            grid=(n_x,),
            in_specs=[
                pl.BlockSpec(activations.shape, lambda i, *_: (0, 0)),
                pl.BlockSpec((tokens, W), lambda i, *_: (0, i)),
                pl.BlockSpec(stats_old.shape, lambda i, *_: (0, 0, 0, 0, 0)),
            ],
            out_specs=pl.BlockSpec((1, SENT, W), lambda i, *_: (i, 0, 0)),
            scratch_shapes=[pltpu.VMEM((rows_dev, tokens), BF)],
        ),
        out_shape=shape((n_x, SENT, W), BF),
        compiler_params=room(32),
    )(where, owners, activations, cotangent, stats_old)
    share = SENT // n_zl
    column = call(sum_kernel, shape((1, SENT, W), BF), swap(sent, "x"))
    column, next_acts = lax.optimization_barrier((column, next_acts))
    part = call(sum_kernel, shape((n_zh, share, W), BF), swap(column.reshape(n_zl, share, W), "zl"))
    mine = call(sum_kernel, shape((n_zl, share, W), BF), swap(part, "zh"))
    full = swap(mine, "zl").reshape(SENT, W)
    others = [next_acts] + [turn(next_acts, "x", k) for k in range(1, n_x)]
    moved, partial_next = pl.pallas_call(
        root_kernel,
        grid_spec=pltpu.PrefetchScalarGridSpec(
            num_scalar_prefetch=1,
            grid=(1,),
            in_specs=[
                pl.BlockSpec((SENT, W), lambda i, where: (0, 0)),
                pl.BlockSpec((rows_dev, W), lambda i, where: (0, where[2])),
                *[pl.BlockSpec((tokens, rows_dev), lambda i, where: (0, 0))] * n_x,
            ],
            out_specs=[
                pl.BlockSpec((4 * W, W), lambda i, where: (0, 0)),
                pl.BlockSpec((n_x * W, tokens), lambda i, where: (0, 0)),
            ],
        ),
        out_shape=[shape((4 * W, W), BF), shape((n_x * W, tokens), BF)],
        compiler_params=room(32),
    )(where, full, weight, *others)
    tiles = swap(partial_next.reshape(n_feat, columns // n_feat, tokens), "feat")
    parts = [moved] + [turn(moved, "x", k) for k in range(1, n_x)]
    weight_new, stats_new = call(
        finish_kernel,
        [shape(weight.shape, F32), shape(stats_old.shape, F32)],
        where,
        owners,
        *parts,
        weight,
        stats_old,
        specs=[IN_SMEM, IN_SMEM] + [IN_VMEM] * 6,
    )
    summed = jnp.sum(tiles.astype(F32), axis=0).astype(BF)
    each = n_feat // n_x
    pairs = [
        (x * n_feat + to * each + j, to * n_feat + x * each + j)
        for x in range(n_x)
        for to in range(n_x)
        for j in range(each)
    ]
    next_out = lax.ppermute(summed, ("x", "feat"), pairs).T
    return (weight_new, stats_new, next_out)


def solution(mesh):
    torus = Mesh(mesh.devices.reshape(4, 3, 4, mesh.shape["feat"]), ("x", "zh", "zl", "feat"))
    return jax.shard_map(
        body,
        mesh=torus,
        in_specs=(
            P(DP, "feat"),
            P(DP, None),
            P("feat", None),
            P("feat", DP, None, None, None),
            P(),
            P(DP, "feat"),
        ),
        out_specs=(P("feat", None), P("feat", DP, None, None, None), P(DP, "feat")),
        check_vma=False,
    )
```

```python
import jax
import jax.numpy as jnp
from jax import lax
from jax.experimental import pallas as pl
from jax.experimental.pallas import tpu as pltpu
from jax.sharding import Mesh
from jax.sharding import PartitionSpec as P

ITERS = 6
DP = ("x", "zh", "zl")
BF = jnp.bfloat16
F32 = jnp.float32
decay_rate = 0.9
step_rate = 0.01

W = 256
H = W // 2
PACK = H + 16
EACH = W + PACK
SENT = 2 * EACH


def room(mib):
    return pltpu.CompilerParams(vmem_limit_bytes=mib * 1024 * 1024)


IN_VMEM = pl.BlockSpec(memory_space=pltpu.VMEM)
IN_HBM = pl.BlockSpec(memory_space=pltpu.HBM)


def dims(rows, cols):
    return (
        lax.broadcasted_iota(jnp.int32, (rows, cols), 0),
        lax.broadcasted_iota(jnp.int32, (rows, cols), 1),
    )


def start_copies(pairs, sems):
    copies = [pltpu.make_async_copy(a, b, sems.at[i]) for i, (a, b) in enumerate(pairs)]
    for copy in copies:
        copy.start()
    return copies


def wide(start):
    return pl.ds(pl.multiple_of(start * W, W), W)


def mine_and_slot(owners, block):
    me = (lax.axis_index("x") * 3 + lax.axis_index("zh")) * 4 + lax.axis_index("zl")
    base = lax.axis_index("feat") * 2
    mine = jnp.int32(0)
    slot = jnp.int32(0)
    for other in range(8):
        held = (owners[other % 4, base + other // 4] == me).astype(jnp.int32)
        slot += jnp.where(other < block, held, 0)
        mine += jnp.where(other == block, held, 0)
    return mine == 1, slot


def pack(old, out, start):
    row, col = dims(H, H)
    upper, lower = old[:H, :H], old[H:, H:]
    out[start : start + H, :H] = old[:H, H:].astype(BF)
    out[start : start + H, H:] = jnp.where(col >= row, upper, lower).astype(BF)
    diagonal = jnp.sum(jnp.where(row == col, lower, 0.0), axis=0, keepdims=True)
    out[start + H : start + PACK, :H] = jnp.broadcast_to(diagonal, (PACK - H, H)).astype(BF)
    out[start + H : start + PACK, H:] = jnp.zeros((PACK - H, H), BF)


def unpack(tile, start):
    row, col = dims(H, H)
    packed = tile[start : start + H, :].astype(F32)
    diagonal = tile[start + H : start + PACK, :H][:1, :].astype(F32)
    flipped = packed.T
    both, both_t = packed[:, H:], flipped[H:, :]
    upper = jnp.where(col >= row, both, both_t)
    lower = jnp.where(col < row, both, jnp.where(col > row, both_t, jnp.broadcast_to(diagonal, (H, H))))
    return jnp.concatenate(
        [
            jnp.concatenate([upper, packed[:, :H]], axis=1),
            jnp.concatenate([flipped[:H, :], lower], axis=1),
        ],
        axis=0,
    )


def grad_kernel(owners_in, acts_in, cot_in, stats_in, out, owners, acts, cot, stats, turned, sems):
    copies = start_copies(
        [(acts_in, acts), (owners_in, owners)]
        + [(cot_in.at[:, i * W : (i + 1) * W], cot.at[:, i * W : (i + 1) * W]) for i in range(4)]
        + [(stats_in.at[0, 0, k], stats.at[k]) for k in range(2)],
        sems,
    )
    for r in range(2):
        for i in range(4):
            out[i, r * EACH + W : (r + 1) * EACH, :] = jnp.zeros((PACK, W), BF)
    copies[0].wait()
    turned[...] = acts[...].T
    for i in range(4):
        copies[2 + i].wait()
        part = jnp.dot(turned[...], cot[:, i * W : (i + 1) * W], preferred_element_type=F32).astype(BF)
        for r in range(2):
            out[i, r * EACH : r * EACH + W, :] = part[r * W : (r + 1) * W, :]
    for at in (1, 6, 7):
        copies[at].wait()
    for r in range(2):
        for i in range(4):
            mine, slot = mine_and_slot(owners, r * 4 + i)

            @pl.when(mine)
            def _(i=i, r=r, slot=slot):
                pack(stats[jnp.minimum(slot, 1)], out.at[i], r * EACH + W)


def sum_kernel(tiles, out):
    total = tiles[0].astype(F32)
    for i in range(1, tiles.shape[0]):
        total += tiles[i].astype(F32)
    total = total.astype(BF)
    for i in range(out.shape[0]):
        out[i] = total


def dot(a, b):
    return jnp.dot(a, b, preferred_element_type=F32)


def root_kernel(tile, weight_in, own, first, second, third, sent, out, weight, acts, sems):
    x = lax.axis_index("x")
    copies = start_copies(
        [(weight_in.at[:, wide(x)], weight)]
        + [(part, acts.at[k]) for k, part in enumerate((own, first, second, third))],
        sems,
    )
    big_row, big_col = dims(W, W)
    identity = (big_row == big_col).astype(F32)
    grads, matrices, iterates, norms = [], [], [], []
    for r in range(2):
        grad = tile[r * EACH : r * EACH + W, :]
        old = unpack(tile, r * EACH + W)
        gram = lax.dot_general(grad, grad, (((1,), (1,)), ((), ())), preferred_element_type=F32) / W
        pack(gram, sent, r * EACH + W)
        renewed = decay_rate * old + (1.0 - decay_rate) * gram
        norm = jnp.sqrt(jnp.sum(renewed * renewed, axis=(0, 1), keepdims=True) + 1e-06)
        grads.append(grad)
        matrices.append(renewed / norm)
        norms.append(norm)
        iterates.append(None)
    for step in range(ITERS):
        for r in range(2):
            low = ((5.0 * identity - matrices[r]) / 4.0).astype(BF)
            if step == 0:
                iterates[r] = low.astype(F32)
            else:
                iterates[r] = dot(iterates[r].astype(BF), low)
            if step + 1 < ITERS:
                square = dot(low, low).astype(BF)
                fourth = dot(square, square).astype(BF)
                matrices[r] = dot(fourth, matrices[r].astype(BF))
    for copy in copies:
        copy.wait()
    news = []
    for r in range(2):
        root = (iterates[r] * lax.rsqrt(jnp.sqrt(norms[r]))).astype(BF)
        update = dot(root, grads[r]).astype(BF)
        sent[r * EACH : r * EACH + W, :] = update
        news.append((weight[r * W : (r + 1) * W, :] - step_rate * update.astype(F32)).astype(BF))
    new = jnp.concatenate(news, axis=0)
    for k in range(4):
        part = lax.dot_general(new, acts[k], (((0,), (1,)), ((), ())), preferred_element_type=F32).astype(BF)
        out[wide((x + (4 - k)) % 4), :] = part


def renew(owners, block, packed, start, stats, stats_new):
    mine, slot = mine_and_slot(owners, block)

    @pl.when(mine)
    def _():
        at = jnp.minimum(slot, 1)
        stats_new[at] = decay_rate * stats[at] + (1.0 - decay_rate) * unpack(packed, start)


def finish_kernel(
    owners_in, own, first, second_top, second_low, third, weight_in, stats_in,
    weight_out, stats_out, owners, weight, stats, new, stats_new, sems, out_sems
):
    x = lax.axis_index("x")
    columns = [(x + (4 - k)) % 4 for k in range(4)]
    copies = start_copies(
        [(owners_in, owners)]
        + [(stats_in.at[0, 0, k], stats.at[k]) for k in range(2)]
        + [(weight_in.at[:, wide(c)], weight.at[k]) for k, c in enumerate(columns)],
        sems,
    )
    halves = [[(own, 0), (own, EACH)], [(first, 0), (first, EACH)], [(second_top, 0), (second_low, 0)], [(third, 0), (third, EACH)]]
    sends = []
    for k in range(4):
        copies[3 + k].wait()
        for r, (part, start) in enumerate(halves[k]):
            rows = slice(r * W, (r + 1) * W)
            new[k, rows, :] = weight[k, rows, :] - step_rate * part[start : start + W, :].astype(F32)
        send = pltpu.make_async_copy(new.at[k], weight_out.at[:, wide(columns[k])], out_sems.at[k])
        send.start()
        sends.append(send)
    for at in range(3):
        copies[at].wait()
    stats_new[...] = jnp.zeros(stats_new.shape, F32)
    for k in range(4):
        for r, (part, start) in enumerate(halves[k]):
            renew(owners, r * 4 + columns[k], part, start + W, stats, stats_new)
    send = pltpu.make_async_copy(stats_new, stats_out.at[0, 0], out_sems.at[4])
    send.start()
    sends.append(send)
    for send in sends:
        send.wait()


def call(kernel, out, *args, specs=None, out_specs=None, scratch=(), mib=32):
    return pl.pallas_call(
        kernel,
        out_shape=out,
        in_specs=specs or [IN_VMEM] * len(args),
        out_specs=out_specs or jax.tree.map(lambda _: IN_VMEM, out),
        scratch_shapes=list(scratch),
        compiler_params=room(mib),
    )(*args)


def swap(x, axis):
    return lax.all_to_all(x, axis, 0, 0, tiled=True)


def turn(x, axis, by):
    n = lax.axis_size(axis)
    return lax.ppermute(x, axis, [(i, (i + by) % n) for i in range(n)])


def body(activations, cotangent, weight, stats_old, owners, next_acts):
    n_x, n_zh, n_zl, n_feat = (lax.axis_size(a) for a in ("x", "zh", "zl", "feat"))
    rows_dev, columns = weight.shape
    tokens = activations.shape[0]
    owners = owners.T
    shape = jax.ShapeDtypeStruct
    dma = pltpu.SemaphoreType.DMA
    sent = call(
        grad_kernel,
        shape((n_x, SENT, W), BF),
        owners,
        activations,
        cotangent,
        stats_old,
        specs=[IN_HBM] * 4,
        scratch=[
            pltpu.SMEM(owners.shape, jnp.int32),
            pltpu.VMEM((tokens, rows_dev), BF),
            pltpu.VMEM((tokens, columns), BF),
            pltpu.VMEM((2, W, W), F32),
            pltpu.VMEM((rows_dev, tokens), BF),
            dma((8,)),
        ],
        mib=60,
    )
    share = SENT // n_zl
    column = call(sum_kernel, shape((1, SENT, W), BF), swap(sent, "x"))
    column, acts = lax.optimization_barrier((column, next_acts))
    acts_1, acts_3 = turn(acts, "x", 1), turn(acts, "x", 3)
    tiles = swap(column.reshape(n_zl, share, W), "zl")
    tiles, acts, acts_1, acts_3 = lax.optimization_barrier((tiles, next_acts, acts_1, acts_3))
    part = call(sum_kernel, shape((n_zh, share, W), BF), tiles)
    part, acts = lax.optimization_barrier((part, acts))
    acts_2 = turn(acts, "x", 2)
    tiles = swap(part, "zh")
    tiles, acts_2 = lax.optimization_barrier((tiles, acts_2))
    mine = call(sum_kernel, shape((n_zl, share, W), BF), tiles)
    full = swap(mine, "zl").reshape(SENT, W)
    moved, partial_next = call(
        root_kernel,
        [shape((SENT, W), BF), shape((n_x * W, tokens), BF)],
        full,
        weight,
        next_acts,
        acts_1,
        acts_2,
        acts_3,
        specs=[IN_VMEM] + [IN_HBM] * 5,
        scratch=[pltpu.VMEM((rows_dev, W), F32), pltpu.VMEM((n_x, tokens, rows_dev), BF), dma((5,))],
    )
    tiles = swap(partial_next.reshape(n_feat, columns // n_feat, tokens), "feat")
    moved_1, moved_3 = turn(moved, "x", 1), turn(moved, "x", 3)
    moved_2 = turn(moved_1[:EACH], "x", 1), turn(moved_3[EACH:], "x", 3)
    weight_new, stats_new = call(
        finish_kernel,
        [shape(weight.shape, F32), shape(stats_old.shape, F32)],
        owners,
        moved,
        moved_1,
        *moved_2,
        moved_3,
        weight,
        stats_old,
        specs=[IN_HBM] + [IN_VMEM] * 5 + [IN_HBM] * 2,
        out_specs=[IN_HBM, IN_HBM],
        scratch=[
            pltpu.SMEM(owners.shape, jnp.int32),
            pltpu.VMEM((n_x, rows_dev, W), F32),
            pltpu.VMEM((2, W, W), F32),
            pltpu.VMEM((n_x, rows_dev, W), F32),
            pltpu.VMEM((2, W, W), F32),
            dma((7,)),
            dma((5,)),
        ],
    )
    summed = jnp.sum(tiles.astype(F32), axis=0).astype(BF)
    each = n_feat // n_x
    pairs = [
        (x * n_feat + to * each + j, to * n_feat + x * each + j)
        for x in range(n_x)
        for to in range(n_x)
        for j in range(each)
    ]
    next_out = lax.ppermute(summed, ("x", "feat"), pairs).T
    return (weight_new, stats_new, next_out)


def solution(mesh):
    torus = Mesh(mesh.devices.reshape(4, 3, 4, mesh.shape["feat"]), ("x", "zh", "zl", "feat"))
    return jax.shard_map(
        body,
        mesh=torus,
        in_specs=(
            P(DP, "feat"),
            P(DP, None),
            P("feat", None),
            P("feat", DP, None, None, None),
            P(),
            P(DP, "feat"),
        ),
        out_specs=(P("feat", None), P("feat", DP, None, None, None), P(DP, "feat")),
        check_vma=False,
    )
```

```python
import jax
import jax.numpy as jnp
from jax import lax
from jax.experimental import pallas as pl
from jax.experimental.pallas import tpu as pltpu
from jax.sharding import Mesh
from jax.sharding import PartitionSpec as P

ITERS = 6
DP = ("x", "zh", "zl")
BF = jnp.bfloat16
F32 = jnp.float32
decay_rate = 0.9
step_rate = 0.01

W = 256
H = W // 2
PACK = H + 16
EACH = W + PACK
SENT = 2 * EACH


def room(mib):
    return pltpu.CompilerParams(vmem_limit_bytes=mib * 1024 * 1024)


IN_VMEM = pl.BlockSpec(memory_space=pltpu.VMEM)
IN_HBM = pl.BlockSpec(memory_space=pltpu.HBM)


def dims(rows, cols):
    return (
        lax.broadcasted_iota(jnp.int32, (rows, cols), 0),
        lax.broadcasted_iota(jnp.int32, (rows, cols), 1),
    )


def start_copies(pairs, sems):
    copies = [pltpu.make_async_copy(a, b, sems.at[i]) for i, (a, b) in enumerate(pairs)]
    for copy in copies:
        copy.start()
    return copies


def wide(start):
    return pl.ds(pl.multiple_of(start * W, W), W)


def mine_and_slot(owners, block):
    me = (lax.axis_index("x") * 3 + lax.axis_index("zh")) * 4 + lax.axis_index("zl")
    base = lax.axis_index("feat") * 2
    mine = jnp.int32(0)
    slot = jnp.int32(0)
    for other in range(8):
        held = (owners[other % 4, base + other // 4] == me).astype(jnp.int32)
        slot += jnp.where(other < block, held, 0)
        mine += jnp.where(other == block, held, 0)
    return mine == 1, slot


def pack(old, out, start):
    row, col = dims(H, H)
    upper, lower = old[:H, :H], old[H:, H:]
    out[start : start + H, :H] = old[:H, H:].astype(BF)
    out[start : start + H, H:] = jnp.where(col >= row, upper, lower).astype(BF)
    diagonal = jnp.sum(jnp.where(row == col, lower, 0.0), axis=0, keepdims=True)
    out[start + H : start + PACK, :H] = jnp.broadcast_to(diagonal, (PACK - H, H)).astype(BF)
    out[start + H : start + PACK, H:] = jnp.zeros((PACK - H, H), BF)


def unpack(tile, start):
    row, col = dims(H, H)
    packed = tile[start : start + H, :].astype(F32)
    diagonal = tile[start + H : start + PACK, :H][:1, :].astype(F32)
    flipped = packed.T
    both, both_t = packed[:, H:], flipped[H:, :]
    upper = jnp.where(col >= row, both, both_t)
    lower = jnp.where(col < row, both, jnp.where(col > row, both_t, jnp.broadcast_to(diagonal, (H, H))))
    return jnp.concatenate(
        [
            jnp.concatenate([upper, packed[:, :H]], axis=1),
            jnp.concatenate([flipped[:H, :], lower], axis=1),
        ],
        axis=0,
    )


def grad_kernel(owners_in, acts_in, cot_in, stats_in, sent, owners, acts, cot, stats, turned, out, sems, out_sems):
    copies = start_copies(
        [(acts_in, acts), (owners_in, owners)]
        + [(cot_in.at[:, i * W : (i + 1) * W], cot.at[:, i * W : (i + 1) * W]) for i in range(4)]
        + [(stats_in.at[0, 0, k], stats.at[k]) for k in range(2)],
        sems,
    )
    for r in range(2):
        for i in range(4):
            out[i, r * EACH + W : (r + 1) * EACH, :] = jnp.zeros((PACK, W), BF)
    for at in (1, 6, 7, 0):
        copies[at].wait()
    turned[...] = acts[...].T
    sends = []
    for i in range(4):
        copies[2 + i].wait()
        part = jnp.dot(turned[...], cot[:, i * W : (i + 1) * W], preferred_element_type=F32).astype(BF)
        for r in range(2):
            out[i, r * EACH : r * EACH + W, :] = part[r * W : (r + 1) * W, :]
            mine, slot = mine_and_slot(owners, r * 4 + i)

            @pl.when(mine)
            def _(i=i, r=r, slot=slot):
                pack(stats[jnp.minimum(slot, 1)], out.at[i], r * EACH + W)

        sends.append(pltpu.make_async_copy(out.at[i], sent.at[i], out_sems.at[i]))
        sends[-1].start()
    for send in sends:
        send.wait()


def sum_kernel(tiles, out):
    total = tiles[0].astype(F32)
    for i in range(1, tiles.shape[0]):
        total += tiles[i].astype(F32)
    total = total.astype(BF)
    for i in range(out.shape[0]):
        out[i] = total


def dot(a, b):
    return jnp.dot(a, b, preferred_element_type=F32)


def root_kernel(tile, updates, products):
    big_row, big_col = dims(W, W)
    identity = (big_row == big_col).astype(F32)
    grads, matrices, iterates, norms = [], [], [], []
    for r in range(2):
        grad = tile[r * EACH : r * EACH + W, :]
        old = unpack(tile, r * EACH + W)
        gram = lax.dot_general(grad, grad, (((1,), (1,)), ((), ())), preferred_element_type=F32) / W
        pack(gram, products, r * PACK)
        renewed = decay_rate * old + (1.0 - decay_rate) * gram
        norm = jnp.sqrt(jnp.sum(renewed * renewed, axis=(0, 1), keepdims=True) + 1e-06)
        grads.append(grad)
        matrices.append(renewed / norm)
        norms.append(norm)
        iterates.append(None)
    for step in range(ITERS):
        for r in range(2):
            low = ((5.0 * identity - matrices[r]) / 4.0).astype(BF)
            if step == 0:
                iterates[r] = low.astype(F32)
            else:
                iterates[r] = dot(iterates[r].astype(BF), low)
            if step + 1 < ITERS:
                square = dot(low, low).astype(BF)
                fourth = dot(square, square).astype(BF)
                matrices[r] = dot(fourth, matrices[r].astype(BF))
    for r in range(2):
        root = (iterates[r] * lax.rsqrt(jnp.sqrt(norms[r]))).astype(BF)
        update = dot(root, grads[r]).astype(BF)
        for i in range(updates.shape[0]):
            updates[i, r * W : (r + 1) * W, :] = update


def next_kernel(weight, updates, acts, out, parts, sems):
    sends = []
    for i in range(4):
        new = weight[:, i * W : (i + 1) * W] - step_rate * updates[i].astype(F32)
        parts[i] = lax.dot_general(
            new.astype(BF), acts[...], (((0,), (1,)), ((), ())), preferred_element_type=F32
        ).astype(BF)
        sends.append(pltpu.make_async_copy(parts.at[i], out.at[i], sems.at[i]))
        sends[-1].start()
    for send in sends:
        send.wait()


def weight_kernel(weight, updates, weight_new):
    weight_new[...] = weight[...] - step_rate * updates[0].astype(F32)


def stats_kernel(owners_in, own, first, second, third, stats_in, stats_new, owners, stats, sems):
    x = lax.axis_index("x")
    copies = start_copies(
        [(owners_in, owners)] + [(stats_in.at[0, 0, k], stats.at[k]) for k in range(2)],
        sems,
    )
    stats_new[...] = jnp.zeros(stats_new.shape, F32)
    for copy in copies:
        copy.wait()
    for k, part in enumerate((own, first, second, third)):
        for r in range(2):
            mine, slot = mine_and_slot(owners, r * 4 + (x + (4 - k)) % 4)

            @pl.when(mine)
            def _(r=r, part=part, slot=slot):
                at = jnp.minimum(slot, 1)
                stats_new[0, 0, at] = decay_rate * stats[at] + (1.0 - decay_rate) * unpack(part, r * PACK)


def call(kernel, out, *args, specs=None, out_specs=None, scratch=(), mib=32):
    return pl.pallas_call(
        kernel,
        out_shape=out,
        in_specs=specs or [IN_VMEM] * len(args),
        out_specs=out_specs or jax.tree.map(lambda _: IN_VMEM, out),
        scratch_shapes=list(scratch),
        compiler_params=room(mib),
    )(*args)


def swap(x, axis):
    return lax.all_to_all(x, axis, 0, 0, tiled=True)


def turn(x, axis, by):
    n = lax.axis_size(axis)
    return lax.ppermute(x, axis, [(i, (i + by) % n) for i in range(n)])


def body(activations, cotangent, weight, stats_old, owners, next_acts):
    n_x, n_zh, n_zl, n_feat = (lax.axis_size(a) for a in ("x", "zh", "zl", "feat"))
    rows_dev, columns = weight.shape
    tokens = activations.shape[0]
    owners = owners.T
    shape = jax.ShapeDtypeStruct
    dma = pltpu.SemaphoreType.DMA
    sent = call(
        grad_kernel,
        shape((n_x, SENT, W), BF),
        owners,
        activations,
        cotangent,
        stats_old,
        specs=[IN_HBM] * 4,
        scratch=[
            pltpu.SMEM(owners.shape, jnp.int32),
            pltpu.VMEM((tokens, rows_dev), BF),
            pltpu.VMEM((tokens, columns), BF),
            pltpu.VMEM((2, W, W), F32),
            pltpu.VMEM((rows_dev, tokens), BF),
            pltpu.VMEM((n_x, SENT, W), BF),
            dma((8,)),
            dma((n_x,)),
        ],
        out_specs=IN_HBM,
        mib=60,
    )
    share = SENT // n_zl
    column = call(sum_kernel, shape((1, SENT, W), BF), swap(sent, "x"))
    part = call(sum_kernel, shape((n_zh, share, W), BF), swap(column.reshape(n_zl, share, W), "zl"))
    mine = call(sum_kernel, shape((n_zl, share, W), BF), swap(part, "zh"))
    full = swap(mine, "zl").reshape(SENT, W)
    updates, products = call(root_kernel, [shape((n_x, rows_dev, W), BF), shape((2 * PACK, W), BF)], full)
    updates = swap(updates, "x")
    partial_next = call(
        next_kernel,
        shape((n_x, W, tokens), BF),
        weight,
        updates,
        next_acts,
        out_specs=IN_HBM,
        scratch=[pltpu.VMEM((n_x, W, tokens), BF), dma((n_x,))],
    )
    partial_next, products = lax.optimization_barrier((partial_next, products))
    tiles = swap(partial_next.reshape(n_feat, columns // n_feat, tokens), "feat")
    weight_new = pl.pallas_call(
        weight_kernel,
        grid=(n_x,),
        in_specs=[
            pl.BlockSpec((rows_dev, W), lambda i: (0, i)),
            pl.BlockSpec((1, rows_dev, W), lambda i: (i, 0, 0)),
        ],
        out_specs=pl.BlockSpec((rows_dev, W), lambda i: (0, i)),
        out_shape=shape(weight.shape, F32),
        compiler_params=room(32),
    )(weight, updates)
    stats_new = call(
        stats_kernel,
        shape(stats_old.shape, F32),
        owners,
        products,
        *[turn(products, "x", k) for k in range(1, n_x)],
        stats_old,
        specs=[IN_HBM] + [IN_VMEM] * 4 + [IN_HBM],
        scratch=[pltpu.SMEM(owners.shape, jnp.int32), pltpu.VMEM((2, W, W), F32), dma((3,))],
    )
    next_out = jnp.sum(tiles.astype(F32), axis=0).astype(BF).T
    return (weight_new, stats_new, next_out)


def solution(mesh):
    torus = Mesh(mesh.devices.reshape(4, 3, 4, mesh.shape["feat"]), ("x", "zh", "zl", "feat"))
    return jax.shard_map(
        body,
        mesh=torus,
        in_specs=(
            P(DP, "feat"),
            P(DP, None),
            P("feat", None),
            P("feat", DP, None, None, None),
            P(),
            P(DP, "feat"),
        ),
        out_specs=(P("feat", None), P("feat", DP, None, None, None), P(DP, "feat")),
        check_vma=False,
    )
```

```python
import jax
import jax.numpy as jnp
from jax import lax
from jax.experimental import pallas as pl
from jax.experimental.pallas import tpu as pltpu
from jax.sharding import Mesh
from jax.sharding import PartitionSpec as P

ITERS = 6
DP = ("x", "zh", "zl")
BF = jnp.bfloat16
F32 = jnp.float32
decay_rate = 0.9
step_rate = 0.01

W = 256
H = W // 2
PACK = H + 16
EACH = W + PACK
SENT = 2 * EACH


def room(mib):
    return pltpu.CompilerParams(vmem_limit_bytes=mib * 1024 * 1024)


IN_VMEM = pl.BlockSpec(memory_space=pltpu.VMEM)
IN_HBM = pl.BlockSpec(memory_space=pltpu.HBM)


def dims(rows, cols):
    return (
        lax.broadcasted_iota(jnp.int32, (rows, cols), 0),
        lax.broadcasted_iota(jnp.int32, (rows, cols), 1),
    )


def start_copies(pairs, sems):
    copies = [pltpu.make_async_copy(a, b, sems.at[i]) for i, (a, b) in enumerate(pairs)]
    for copy in copies:
        copy.start()
    return copies


def wide(start):
    return pl.ds(pl.multiple_of(start * W, W), W)


def mine_and_slot(owners, block):
    me = (lax.axis_index("x") * 3 + lax.axis_index("zh")) * 4 + lax.axis_index("zl")
    base = lax.axis_index("feat") * 2
    mine = jnp.int32(0)
    slot = jnp.int32(0)
    for other in range(8):
        held = (owners[other % 4, base + other // 4] == me).astype(jnp.int32)
        slot += jnp.where(other < block, held, 0)
        mine += jnp.where(other == block, held, 0)
    return mine == 1, slot


def pack(old, out, start):
    row, col = dims(H, H)
    upper, lower = old[:H, :H], old[H:, H:]
    out[start : start + H, :H] = old[:H, H:].astype(BF)
    out[start : start + H, H:] = jnp.where(col >= row, upper, lower).astype(BF)
    diagonal = jnp.sum(jnp.where(row == col, lower, 0.0), axis=0, keepdims=True)
    out[start + H : start + PACK, :H] = jnp.broadcast_to(diagonal, (PACK - H, H)).astype(BF)
    out[start + H : start + PACK, H:] = jnp.zeros((PACK - H, H), BF)


def unpack(tile, start):
    row, col = dims(H, H)
    packed = tile[start : start + H, :].astype(F32)
    diagonal = tile[start + H : start + PACK, :H][:1, :].astype(F32)
    flipped = packed.T
    both, both_t = packed[:, H:], flipped[H:, :]
    upper = jnp.where(col >= row, both, both_t)
    lower = jnp.where(col < row, both, jnp.where(col > row, both_t, jnp.broadcast_to(diagonal, (H, H))))
    return jnp.concatenate(
        [
            jnp.concatenate([upper, packed[:, :H]], axis=1),
            jnp.concatenate([flipped[:H, :], lower], axis=1),
        ],
        axis=0,
    )


def grad_kernel(owners_in, acts_in, cot_in, stats_in, sent, owners, acts, cot, stats, turned, out, sems, out_sems):
    copies = start_copies(
        [(acts_in, acts), (owners_in, owners)]
        + [(cot_in.at[:, i * W : (i + 1) * W], cot.at[:, i * W : (i + 1) * W]) for i in range(4)]
        + [(stats_in.at[0, 0, k], stats.at[k]) for k in range(2)],
        sems,
    )
    for r in range(2):
        for i in range(4):
            out[i, r * EACH + W : (r + 1) * EACH, :] = jnp.zeros((PACK, W), BF)
    for at in (1, 6, 7, 0):
        copies[at].wait()
    turned[...] = acts[...].T
    sends = []
    for i in range(4):
        copies[2 + i].wait()
        part = jnp.dot(turned[...], cot[:, i * W : (i + 1) * W], preferred_element_type=F32).astype(BF)
        for r in range(2):
            out[i, r * EACH : r * EACH + W, :] = part[r * W : (r + 1) * W, :]
            mine, slot = mine_and_slot(owners, r * 4 + i)

            @pl.when(mine)
            def _(i=i, r=r, slot=slot):
                pack(stats[jnp.minimum(slot, 1)], out.at[i], r * EACH + W)

        sends.append(pltpu.make_async_copy(out.at[i], sent.at[i], out_sems.at[i]))
        sends[-1].start()
    for send in sends:
        send.wait()


def sum_kernel(tiles, out):
    total = tiles[0].astype(F32)
    for i in range(1, tiles.shape[0]):
        total += tiles[i].astype(F32)
    total = total.astype(BF)
    for i in range(out.shape[0]):
        out[i] = total


def dot(a, b):
    return jnp.dot(a, b, preferred_element_type=F32)


def root_kernel(tile, weight_in, own, first, second, third, sent, out, weight, acts, sems):
    x = lax.axis_index("x")
    copies = start_copies(
        [(weight_in.at[:, wide(x)], weight)]
        + [(part, acts.at[k]) for k, part in enumerate((own, first, second, third))],
        sems,
    )
    big_row, big_col = dims(W, W)
    identity = (big_row == big_col).astype(F32)
    grads, matrices, iterates, norms = [], [], [], []
    for r in range(2):
        grad = tile[r * EACH : r * EACH + W, :]
        old = unpack(tile, r * EACH + W)
        gram = lax.dot_general(grad, grad, (((1,), (1,)), ((), ())), preferred_element_type=F32) / W
        pack(gram, sent, r * EACH + W)
        renewed = decay_rate * old + (1.0 - decay_rate) * gram
        norm = jnp.sqrt(jnp.sum(renewed * renewed, axis=(0, 1), keepdims=True) + 1e-06)
        grads.append(grad)
        matrices.append(renewed / norm)
        norms.append(norm)
        iterates.append(None)
    for step in range(ITERS):
        for r in range(2):
            low = ((5.0 * identity - matrices[r]) / 4.0).astype(BF)
            if step == 0:
                iterates[r] = low.astype(F32)
            else:
                iterates[r] = dot(iterates[r].astype(BF), low)
            if step + 1 < ITERS:
                square = dot(low, low).astype(BF)
                fourth = dot(square, square).astype(BF)
                matrices[r] = dot(fourth, matrices[r].astype(BF))
    for copy in copies:
        copy.wait()
    news = []
    for r in range(2):
        root = (iterates[r] * lax.rsqrt(jnp.sqrt(norms[r]))).astype(BF)
        update = dot(root, grads[r]).astype(BF)
        sent[r * EACH : r * EACH + W, :] = update
        news.append((weight[r * W : (r + 1) * W, :] - step_rate * update.astype(F32)).astype(BF))
    new = jnp.concatenate(news, axis=0)
    for k in range(4):
        part = lax.dot_general(new, acts[k], (((0,), (1,)), ((), ())), preferred_element_type=F32).astype(BF)
        out[wide((x + (4 - k)) % 4), :] = part


def finish_kernel(owners_in, own, first, third, weight_in, stats_in, weight_out, stats_out, owners, weight, stats, new, stats_new, sems, out_sems):
    x = lax.axis_index("x")
    columns = [x, (x + 3) % 4, (x + 1) % 4]
    copies = start_copies(
        [(owners_in, owners)]
        + [(stats_in.at[0, 0, k], stats.at[k]) for k in range(2)]
        + [(weight_in.at[:, wide(c)], weight.at[k]) for k, c in enumerate(columns)],
        sems,
    )
    sends = []
    for k, part in enumerate((own, first, third)):
        copies[3 + k].wait()
        for r in range(2):
            rows = slice(r * W, (r + 1) * W)
            new[k, rows, :] = weight[k, rows, :] - step_rate * part[r * EACH : r * EACH + W, :].astype(F32)
        sends.append(pltpu.make_async_copy(new.at[k], weight_out.at[:, wide(columns[k])], out_sems.at[k]))
        sends[-1].start()
    for at in range(3):
        copies[at].wait()
    stats_new[...] = jnp.zeros(stats_new.shape, F32)
    for k, part in enumerate((own, first, third)):
        for r in range(2):
            mine, slot = mine_and_slot(owners, r * 4 + columns[k])

            @pl.when(mine)
            def _(r=r, part=part, slot=slot):
                at = jnp.minimum(slot, 1)
                stats_new[at] = decay_rate * stats[at] + (1.0 - decay_rate) * unpack(part, r * EACH + W)

    sends.append(pltpu.make_async_copy(stats_new, stats_out.at[0, 0], out_sems.at[3]))
    sends[-1].start()
    for send in sends:
        send.wait()


def last_kernel(owners_in, top, low, weight_in, stats_in, weight_part, stats_part, weight_out, stats_out, owners, weight, stats, new, stats_new, sems, out_sems):
    column = (lax.axis_index("x") + 2) % 4
    copies = start_copies(
        [(owners_in, owners)]
        + [(stats_in.at[0, 0, k], stats.at[k]) for k in range(2)]
        + [(weight_in.at[:, wide(column)], weight)],
        sems,
    )
    copies[3].wait()
    for r, part in enumerate((top, low)):
        rows = slice(r * W, (r + 1) * W)
        new[rows, :] = weight[rows, :] - step_rate * part[:W, :].astype(F32)
    send = pltpu.make_async_copy(new, weight_out.at[:, wide(column)], out_sems.at[0])
    send.start()
    for at in range(3):
        copies[at].wait()
    for r, part in enumerate((top, low)):
        mine, slot = mine_and_slot(owners, r * 4 + column)

        @pl.when(mine)
        def _(r=r, part=part, slot=slot):
            at = jnp.minimum(slot, 1)
            stats_new[...] = decay_rate * stats[at] + (1.0 - decay_rate) * unpack(part, W)
            keep = pltpu.make_async_copy(stats_new, stats_out.at[0, 0, at], out_sems.at[1])
            keep.start()
            keep.wait()

    send.wait()


def call(kernel, out, *args, specs=None, out_specs=None, scratch=(), mib=32, aliases=None):
    return pl.pallas_call(
        kernel,
        out_shape=out,
        in_specs=specs or [IN_VMEM] * len(args),
        out_specs=out_specs or jax.tree.map(lambda _: IN_VMEM, out),
        scratch_shapes=list(scratch),
        input_output_aliases=aliases or {},
        compiler_params=room(mib),
    )(*args)


def swap(x, axis):
    return lax.all_to_all(x, axis, 0, 0, tiled=True)


def turn(x, axis, by):
    n = lax.axis_size(axis)
    return lax.ppermute(x, axis, [(i, (i + by) % n) for i in range(n)])


def body(activations, cotangent, weight, stats_old, owners, next_acts):
    n_x, n_zh, n_zl, n_feat = (lax.axis_size(a) for a in ("x", "zh", "zl", "feat"))
    rows_dev, columns = weight.shape
    tokens = activations.shape[0]
    owners = owners.T
    shape = jax.ShapeDtypeStruct
    dma = pltpu.SemaphoreType.DMA
    sent = call(
        grad_kernel,
        shape((n_x, SENT, W), BF),
        owners,
        activations,
        cotangent,
        stats_old,
        specs=[IN_HBM] * 4,
        scratch=[
            pltpu.SMEM(owners.shape, jnp.int32),
            pltpu.VMEM((tokens, rows_dev), BF),
            pltpu.VMEM((tokens, columns), BF),
            pltpu.VMEM((2, W, W), F32),
            pltpu.VMEM((rows_dev, tokens), BF),
            pltpu.VMEM((n_x, SENT, W), BF),
            dma((8,)),
            dma((n_x,)),
        ],
        out_specs=IN_HBM,
        mib=60,
    )
    share = SENT // n_zl
    column = call(sum_kernel, shape((1, SENT, W), BF), swap(sent, "x"))
    column, acts = lax.optimization_barrier((column, next_acts))
    acts_3 = turn(acts, "x", 3)
    tiles = swap(column.reshape(n_zl, share, W), "zl")
    tiles, acts_3 = lax.optimization_barrier((tiles, acts_3))
    part, acts = lax.optimization_barrier((call(sum_kernel, shape((n_zh, share, W), BF), tiles), acts))
    acts_2 = turn(acts, "x", 2)
    tiles, acts_2 = lax.optimization_barrier((swap(part, "zh"), acts_2))
    mine, acts = lax.optimization_barrier((call(sum_kernel, shape((n_zl, share, W), BF), tiles), acts))
    acts_1 = turn(acts, "x", 1)
    full = swap(mine, "zl").reshape(SENT, W)
    moved, partial_next = call(
        root_kernel,
        [shape((SENT, W), BF), shape((n_x * W, tokens), BF)],
        full,
        weight,
        next_acts,
        acts_1,
        acts_2,
        acts_3,
        specs=[IN_VMEM] + [IN_HBM] * 5,
        scratch=[pltpu.VMEM((rows_dev, W), F32), pltpu.VMEM((n_x, tokens, rows_dev), BF), dma((5,))],
    )
    tiles = swap(partial_next.reshape(n_feat, columns // n_feat, tokens), "feat")
    moved_1, moved_3 = turn(moved, "x", 1), turn(moved, "x", 3)
    moved_2 = turn(moved_1[:EACH], "x", 1), turn(moved_3[EACH:], "x", 3)
    outs = [shape(weight.shape, F32), shape(stats_old.shape, F32)]
    begun = call(
        finish_kernel,
        outs,
        owners,
        moved,
        moved_1,
        moved_3,
        weight,
        stats_old,
        specs=[IN_HBM] + [IN_VMEM] * 3 + [IN_HBM] * 2,
        out_specs=[IN_HBM, IN_HBM],
        scratch=[
            pltpu.SMEM(owners.shape, jnp.int32),
            pltpu.VMEM((3, rows_dev, W), F32),
            pltpu.VMEM((2, W, W), F32),
            pltpu.VMEM((3, rows_dev, W), F32),
            pltpu.VMEM((2, W, W), F32),
            dma((6,)),
            dma((4,)),
        ],
    )
    weight_new, stats_new = call(
        last_kernel,
        outs,
        owners,
        *moved_2,
        weight,
        stats_old,
        *begun,
        specs=[IN_HBM] + [IN_VMEM] * 2 + [IN_HBM] * 4,
        out_specs=[IN_HBM, IN_HBM],
        scratch=[
            pltpu.SMEM(owners.shape, jnp.int32),
            pltpu.VMEM((rows_dev, W), F32),
            pltpu.VMEM((2, W, W), F32),
            pltpu.VMEM((rows_dev, W), F32),
            pltpu.VMEM((W, W), F32),
            dma((4,)),
            dma((2,)),
        ],
        aliases={5: 0, 6: 1},
    )
    summed = jnp.sum(tiles.astype(F32), axis=0).astype(BF)
    each = n_feat // n_x
    pairs = [
        (x * n_feat + to * each + j, to * n_feat + x * each + j)
        for x in range(n_x)
        for to in range(n_x)
        for j in range(each)
    ]
    next_out = lax.ppermute(summed, ("x", "feat"), pairs).T
    return (weight_new, stats_new, next_out)


def solution(mesh):
    torus = Mesh(mesh.devices.reshape(4, 3, 4, mesh.shape["feat"]), ("x", "zh", "zl", "feat"))
    return jax.shard_map(
        body,
        mesh=torus,
        in_specs=(
            P(DP, "feat"),
            P(DP, None),
            P("feat", None),
            P("feat", DP, None, None, None),
            P(),
            P(DP, "feat"),
        ),
        out_specs=(P("feat", None), P("feat", DP, None, None, None), P(DP, "feat")),
        check_vma=False,
    )
```

```python
import jax
import jax.numpy as jnp
from jax import lax
from jax.experimental import pallas as pl
from jax.experimental.pallas import tpu as pltpu
from jax.sharding import Mesh
from jax.sharding import PartitionSpec as P

ITERS = 6
DP = ("x", "zh", "zl")
BF = jnp.bfloat16
F32 = jnp.float32
decay_rate = 0.9
step_rate = 0.01

W = 256
H = W // 2
PACK = H + 16
EACH = W + PACK
SENT = 2 * EACH


def room(mib):
    return pltpu.CompilerParams(vmem_limit_bytes=mib * 1024 * 1024)


IN_VMEM = pl.BlockSpec(memory_space=pltpu.VMEM)
IN_HBM = pl.BlockSpec(memory_space=pltpu.HBM)


def dims(rows, cols):
    return (
        lax.broadcasted_iota(jnp.int32, (rows, cols), 0),
        lax.broadcasted_iota(jnp.int32, (rows, cols), 1),
    )


def start_copies(pairs, sems):
    copies = [pltpu.make_async_copy(a, b, sems.at[i]) for i, (a, b) in enumerate(pairs)]
    for copy in copies:
        copy.start()
    return copies


def wide(start):
    return pl.ds(pl.multiple_of(start * W, W), W)


def mine_and_slot(owners, block):
    me = (lax.axis_index("x") * 3 + lax.axis_index("zh")) * 4 + lax.axis_index("zl")
    base = lax.axis_index("feat") * 2
    mine = jnp.int32(0)
    slot = jnp.int32(0)
    for other in range(8):
        held = (owners[other % 4, base + other // 4] == me).astype(jnp.int32)
        slot += jnp.where(other < block, held, 0)
        mine += jnp.where(other == block, held, 0)
    return mine == 1, slot


def pack(old, out, start):
    row, col = dims(H, H)
    upper, lower = old[:H, :H], old[H:, H:]
    out[start : start + H, :H] = old[:H, H:].astype(BF)
    out[start : start + H, H:] = jnp.where(col >= row, upper, lower).astype(BF)
    diagonal = jnp.sum(jnp.where(row == col, lower, 0.0), axis=0, keepdims=True)
    out[start + H : start + PACK, :H] = jnp.broadcast_to(diagonal, (PACK - H, H)).astype(BF)
    out[start + H : start + PACK, H:] = jnp.zeros((PACK - H, H), BF)


def unpack(tile, start):
    row, col = dims(H, H)
    packed = tile[start : start + H, :].astype(F32)
    diagonal = tile[start + H : start + PACK, :H][:1, :].astype(F32)
    flipped = packed.T
    both, both_t = packed[:, H:], flipped[H:, :]
    upper = jnp.where(col >= row, both, both_t)
    lower = jnp.where(col < row, both, jnp.where(col > row, both_t, jnp.broadcast_to(diagonal, (H, H))))
    return jnp.concatenate(
        [
            jnp.concatenate([upper, packed[:, :H]], axis=1),
            jnp.concatenate([flipped[:H, :], lower], axis=1),
        ],
        axis=0,
    )


def grad_kernel(owners_in, acts_in, cot_in, stats_in, sent, owners, acts, cot, stats, turned, out, sems, out_sems):
    copies = start_copies(
        [(acts_in.at[:, i * H : (i + 1) * H], acts.at[:, i * H : (i + 1) * H]) for i in range(4)]
        + [(cot_in.at[:, i * W : (i + 1) * W], cot.at[:, i * W : (i + 1) * W]) for i in range(4)]
        + [(owners_in, owners)]
        + [(stats_in.at[0, 0, k], stats.at[k]) for k in range(2)],
        sems,
    )
    for r in range(2):
        for i in range(4):
            out[i, r * EACH + W : (r + 1) * EACH, :] = jnp.zeros((PACK, W), BF)
    for i in range(4):
        copies[i].wait()
        turned[i * H : (i + 1) * H, :] = acts[:, i * H : (i + 1) * H].T
    for at in (8, 9, 10):
        copies[at].wait()
    sends = []
    for i in range(4):
        copies[4 + i].wait()
        part = jnp.dot(turned[...], cot[:, i * W : (i + 1) * W], preferred_element_type=F32).astype(BF)
        for r in range(2):
            out[i, r * EACH : r * EACH + W, :] = part[r * W : (r + 1) * W, :]
            mine, slot = mine_and_slot(owners, r * 4 + i)

            @pl.when(mine)
            def _(i=i, r=r, slot=slot):
                pack(stats[jnp.minimum(slot, 1)], out.at[i], r * EACH + W)

        for r in range(2):
            rows = pl.ds(r * EACH, EACH)
            sends.append(pltpu.make_async_copy(out.at[i, rows], sent.at[i, rows], out_sems.at[2 * i + r]))
            sends[-1].start()
    for send in sends:
        send.wait()


def sum_kernel(tiles, out):
    total = tiles[0].astype(F32)
    for i in range(1, tiles.shape[0]):
        total += tiles[i].astype(F32)
    total = total.astype(BF)
    for i in range(out.shape[0]):
        out[i] = total


def dot(a, b):
    return jnp.dot(a, b, preferred_element_type=F32)


def root_kernel(tile, weight_in, own, first, second, third, sent, out, weight, acts, sems):
    x = lax.axis_index("x")
    copies = start_copies(
        [(weight_in.at[:, wide(x)], weight)]
        + [(part, acts.at[k]) for k, part in enumerate((own, first, second, third))],
        sems,
    )
    big_row, big_col = dims(W, W)
    identity = (big_row == big_col).astype(F32)
    grads, matrices, iterates, norms = [], [], [], []
    for r in range(2):
        grad = tile[r * EACH : r * EACH + W, :]
        old = unpack(tile, r * EACH + W)
        gram = lax.dot_general(grad, grad, (((1,), (1,)), ((), ())), preferred_element_type=F32) / W
        pack(gram, sent, r * EACH + W)
        renewed = decay_rate * old + (1.0 - decay_rate) * gram
        norm = jnp.sqrt(jnp.sum(renewed * renewed, axis=(0, 1), keepdims=True) + 1e-06)
        grads.append(grad)
        matrices.append(renewed / norm)
        norms.append(norm)
        iterates.append(None)
    for step in range(ITERS):
        for r in range(2):
            low = ((5.0 * identity - matrices[r]) / 4.0).astype(BF)
            if step == 0:
                iterates[r] = low.astype(F32)
            else:
                iterates[r] = dot(iterates[r].astype(BF), low)
            if step + 1 < ITERS:
                square = dot(low, low).astype(BF)
                fourth = dot(square, square).astype(BF)
                matrices[r] = dot(fourth, matrices[r].astype(BF))
    for copy in copies:
        copy.wait()
    news = []
    for r in range(2):
        root = (iterates[r] * lax.rsqrt(jnp.sqrt(norms[r]))).astype(BF)
        update = dot(root, grads[r]).astype(BF)
        sent[r * EACH : r * EACH + W, :] = update
        news.append((weight[r * W : (r + 1) * W, :] - step_rate * update.astype(F32)).astype(BF))
    new = jnp.concatenate(news, axis=0)
    for k in range(4):
        part = lax.dot_general(new, acts[k], (((0,), (1,)), ((), ())), preferred_element_type=F32).astype(BF)
        out[(x + (4 - k)) % 4] = part


def renewed_weight(halves, weight, new, out, sem):
    for r, (part, start) in enumerate(halves):
        rows = slice(r * W, (r + 1) * W)
        new[rows, :] = weight[rows, :] - step_rate * part[start : start + W, :].astype(F32)
    send = pltpu.make_async_copy(new, out, sem)
    send.start()
    return send


def finish_kernel(owners_in, own, third, weight_in, stats_in, weight_out, stats_out, owners, weight, stats, new, stats_new, sems, out_sems):
    x = lax.axis_index("x")
    columns = [x, (x + 1) % 4]
    copies = start_copies(
        [(owners_in, owners)]
        + [(stats_in.at[0, 0, k], stats.at[k]) for k in range(2)]
        + [(weight_in.at[:, wide(c)], weight.at[k]) for k, c in enumerate(columns)],
        sems,
    )
    sends = []
    for k, part in enumerate((own, third)):
        copies[3 + k].wait()
        halves = (part, 0), (part, EACH)
        sends.append(renewed_weight(halves, weight.at[k], new.at[k], weight_out.at[:, wide(columns[k])], out_sems.at[k]))
    for at in range(3):
        copies[at].wait()
    stats_new[...] = jnp.zeros(stats_new.shape, F32)
    for k, part in enumerate((own, third)):
        for r in range(2):
            mine, slot = mine_and_slot(owners, r * 4 + columns[k])

            @pl.when(mine)
            def _(r=r, part=part, slot=slot):
                at = jnp.minimum(slot, 1)
                stats_new[at] = decay_rate * stats[at] + (1.0 - decay_rate) * unpack(part, r * EACH + W)

    sends.append(pltpu.make_async_copy(stats_new, stats_out.at[0, 0], out_sems.at[2]))
    sends[-1].start()
    for send in sends:
        send.wait()


def last_kernel(owners_in, first, top, low, weight_in, stats_in, weight_part, stats_part, weight_out, stats_out, owners, weight, stats, new, stats_new, sems, out_sems):
    x = lax.axis_index("x")
    columns = [(x + 3) % 4, (x + 2) % 4]
    copies = start_copies(
        [(owners_in, owners)]
        + [(stats_in.at[0, 0, k], stats.at[k]) for k in range(2)]
        + [(weight_in.at[:, wide(c)], weight.at[k]) for k, c in enumerate(columns)],
        sems,
    )
    blocks = [[(first, 0), (first, EACH)], [(top, 0), (low, 0)]]
    sends = []
    for k, halves in enumerate(blocks):
        copies[3 + k].wait()
        sends.append(renewed_weight(halves, weight.at[k], new.at[k], weight_out.at[:, wide(columns[k])], out_sems.at[k]))
    for at in range(3):
        copies[at].wait()
    for k, halves in enumerate(blocks):
        for r, (part, start) in enumerate(halves):
            mine, slot = mine_and_slot(owners, r * 4 + columns[k])

            @pl.when(mine)
            def _(part=part, start=start, slot=slot):
                at = jnp.minimum(slot, 1)
                stats_new[...] = decay_rate * stats[at] + (1.0 - decay_rate) * unpack(part, start + W)
                keep = pltpu.make_async_copy(stats_new, stats_out.at[0, 0, at], out_sems.at[2])
                keep.start()
                keep.wait()

    for send in sends:
        send.wait()


def call(kernel, out, *args, specs=None, out_specs=None, scratch=(), mib=32, aliases=None):
    return pl.pallas_call(
        kernel,
        out_shape=out,
        in_specs=specs or [IN_VMEM] * len(args),
        out_specs=out_specs or jax.tree.map(lambda _: IN_VMEM, out),
        scratch_shapes=list(scratch),
        input_output_aliases=aliases or {},
        compiler_params=room(mib),
    )(*args)


def swap(x, axis):
    return lax.all_to_all(x, axis, 0, 0, tiled=True)


def turn(x, axis, by):
    n = lax.axis_size(axis)
    return lax.ppermute(x, axis, [(i, (i + by) % n) for i in range(n)])


def body(activations, cotangent, weight, stats_old, owners, next_acts):
    n_x, n_zh, n_zl, n_feat = (lax.axis_size(a) for a in ("x", "zh", "zl", "feat"))
    rows_dev, columns = weight.shape
    tokens = activations.shape[0]
    owners = owners.T
    shape = jax.ShapeDtypeStruct
    dma = pltpu.SemaphoreType.DMA
    sent = call(
        grad_kernel,
        shape((n_x, SENT, W), BF),
        owners,
        activations,
        cotangent,
        stats_old,
        specs=[IN_HBM] * 4,
        scratch=[
            pltpu.SMEM(owners.shape, jnp.int32),
            pltpu.VMEM((tokens, rows_dev), BF),
            pltpu.VMEM((tokens, columns), BF),
            pltpu.VMEM((2, W, W), F32),
            pltpu.VMEM((rows_dev, tokens), BF),
            pltpu.VMEM((n_x, SENT, W), BF),
            dma((11,)),
            dma((2 * n_x,)),
        ],
        out_specs=IN_HBM,
        mib=60,
    )
    share = SENT // n_zl
    column = call(sum_kernel, shape((1, SENT, W), BF), swap(sent, "x"))
    column, acts = lax.optimization_barrier((column, next_acts))
    acts_3 = turn(acts, "x", 3)
    tiles = swap(column.reshape(n_zl, share, W), "zl")
    tiles, acts_3 = lax.optimization_barrier((tiles, acts_3))
    part, acts = lax.optimization_barrier((call(sum_kernel, shape((n_zh, share, W), BF), tiles), acts))
    acts_2 = turn(acts, "x", 2)
    tiles, acts_2 = lax.optimization_barrier((swap(part, "zh"), acts_2))
    mine, acts = lax.optimization_barrier((call(sum_kernel, shape((n_zl, share, W), BF), tiles), acts))
    acts_1 = turn(acts, "x", 1)
    full = swap(mine, "zl").reshape(SENT, W)
    moved, partial_next = call(
        root_kernel,
        [shape((SENT, W), BF), shape((n_x, W, tokens), BF)],
        full,
        weight,
        next_acts,
        acts_1,
        acts_2,
        acts_3,
        specs=[IN_VMEM] + [IN_HBM] * 5,
        scratch=[pltpu.VMEM((rows_dev, W), F32), pltpu.VMEM((n_x, tokens, rows_dev), BF), dma((5,))],
        mib=60,
    )
    tiles = swap(partial_next.reshape(n_feat, columns // n_feat, tokens), "feat")
    moved_3, moved_2, moved_1 = turn(moved, "x", 3), turn(moved[:EACH], "x", 2), turn(moved, "x", 1)
    moved_2 = moved_2, turn(moved_3[EACH:], "x", 3)
    outs = [shape(weight.shape, F32), shape(stats_old.shape, F32)]
    begun = call(
        finish_kernel,
        outs,
        owners,
        moved,
        moved_3,
        weight,
        stats_old,
        specs=[IN_HBM] + [IN_VMEM] * 2 + [IN_HBM] * 2,
        out_specs=[IN_HBM, IN_HBM],
        scratch=[
            pltpu.SMEM(owners.shape, jnp.int32),
            pltpu.VMEM((2, rows_dev, W), F32),
            pltpu.VMEM((2, W, W), F32),
            pltpu.VMEM((2, rows_dev, W), F32),
            pltpu.VMEM((2, W, W), F32),
            dma((5,)),
            dma((3,)),
        ],
    )
    weight_new, stats_new = call(
        last_kernel,
        outs,
        owners,
        moved_1,
        *moved_2,
        weight,
        stats_old,
        *begun,
        specs=[IN_HBM] + [IN_VMEM] * 3 + [IN_HBM] * 4,
        out_specs=[IN_HBM, IN_HBM],
        scratch=[
            pltpu.SMEM(owners.shape, jnp.int32),
            pltpu.VMEM((2, rows_dev, W), F32),
            pltpu.VMEM((2, W, W), F32),
            pltpu.VMEM((2, rows_dev, W), F32),
            pltpu.VMEM((W, W), F32),
            dma((5,)),
            dma((3,)),
        ],
        aliases={6: 0, 7: 1},
    )
    summed = jnp.sum(tiles.astype(F32), axis=0).astype(BF)
    each = n_feat // n_x
    pairs = [
        (x * n_feat + to * each + j, to * n_feat + x * each + j)
        for x in range(n_x)
        for to in range(n_x)
        for j in range(each)
    ]
    next_out = lax.ppermute(summed, ("x", "feat"), pairs).T
    return (weight_new, stats_new, next_out)


def solution(mesh):
    torus = Mesh(mesh.devices.reshape(4, 3, 4, mesh.shape["feat"]), ("x", "zh", "zl", "feat"))
    return jax.shard_map(
        body,
        mesh=torus,
        in_specs=(
            P(DP, "feat"),
            P(DP, None),
            P("feat", None),
            P("feat", DP, None, None, None),
            P(),
            P(DP, "feat"),
        ),
        out_specs=(P("feat", None), P("feat", DP, None, None, None), P(DP, "feat")),
        check_vma=False,
    )
```

```python
import jax
import jax.numpy as jnp
from jax import lax
from jax.experimental import pallas as pl
from jax.experimental.pallas import tpu as pltpu
from jax.sharding import Mesh
from jax.sharding import PartitionSpec as P

ITERS = 6
DP = ("x", "zh", "zl")
BF = jnp.bfloat16
F32 = jnp.float32
decay_rate = 0.9
step_rate = 0.01

W = 256
H = W // 2
PACK = H + 16
EACH = W + PACK
SENT = 2 * EACH


def room(mib):
    return pltpu.CompilerParams(vmem_limit_bytes=mib * 1024 * 1024)


IN_VMEM = pl.BlockSpec(memory_space=pltpu.VMEM)
IN_HBM = pl.BlockSpec(memory_space=pltpu.HBM)


def dims(rows, cols):
    return (
        lax.broadcasted_iota(jnp.int32, (rows, cols), 0),
        lax.broadcasted_iota(jnp.int32, (rows, cols), 1),
    )


def start_copies(pairs, sems):
    copies = [pltpu.make_async_copy(a, b, sems.at[i]) for i, (a, b) in enumerate(pairs)]
    for copy in copies:
        copy.start()
    return copies


def wide(start):
    return pl.ds(pl.multiple_of(start * W, W), W)


def mine_and_slot(owners, block):
    me = (lax.axis_index("x") * 3 + lax.axis_index("zh")) * 4 + lax.axis_index("zl")
    base = lax.axis_index("feat") * 2
    mine = jnp.int32(0)
    slot = jnp.int32(0)
    for other in range(8):
        held = (owners[other % 4, base + other // 4] == me).astype(jnp.int32)
        slot += jnp.where(other < block, held, 0)
        mine += jnp.where(other == block, held, 0)
    return mine == 1, slot


def pack(old, out, start):
    row, col = dims(H, H)
    upper, lower = old[:H, :H], old[H:, H:]
    out[start : start + H, :H] = old[:H, H:].astype(BF)
    out[start : start + H, H:] = jnp.where(col >= row, upper, lower).astype(BF)
    diagonal = jnp.sum(jnp.where(row == col, lower, 0.0), axis=0, keepdims=True)
    out[start + H : start + PACK, :H] = jnp.broadcast_to(diagonal, (PACK - H, H)).astype(BF)
    out[start + H : start + PACK, H:] = jnp.zeros((PACK - H, H), BF)


def unpack(tile, start):
    row, col = dims(H, H)
    packed = tile[start : start + H, :].astype(F32)
    diagonal = tile[start + H : start + PACK, :H][:1, :].astype(F32)
    flipped = packed.T
    both, both_t = packed[:, H:], flipped[H:, :]
    upper = jnp.where(col >= row, both, both_t)
    lower = jnp.where(col < row, both, jnp.where(col > row, both_t, jnp.broadcast_to(diagonal, (H, H))))
    return jnp.concatenate(
        [
            jnp.concatenate([upper, packed[:, :H]], axis=1),
            jnp.concatenate([flipped[:H, :], lower], axis=1),
        ],
        axis=0,
    )


def grad_kernel(owners_in, acts_in, cot_in, stats_in, sent, owners, acts, cot, stats, turned, out, sems, out_sems):
    copies = start_copies(
        [(acts_in.at[:, i * H : (i + 1) * H], acts.at[:, i * H : (i + 1) * H]) for i in range(4)]
        + [(cot_in.at[:, i * W : (i + 1) * W], cot.at[:, i * W : (i + 1) * W]) for i in range(4)]
        + [(owners_in, owners)]
        + [(stats_in.at[0, 0, k], stats.at[k]) for k in range(2)],
        sems,
    )
    for r in range(2):
        for i in range(4):
            out[i, r * EACH + W : (r + 1) * EACH, :] = jnp.zeros((PACK, W), BF)
    for i in range(4):
        copies[i].wait()
        turned[i * H : (i + 1) * H, :] = acts[:, i * H : (i + 1) * H].T
    for at in (8, 9, 10):
        copies[at].wait()
    sends = []
    for i in range(4):
        copies[4 + i].wait()
        part = jnp.dot(turned[...], cot[:, i * W : (i + 1) * W], preferred_element_type=F32).astype(BF)
        for r in range(2):
            out[i, r * EACH : r * EACH + W, :] = part[r * W : (r + 1) * W, :]
            mine, slot = mine_and_slot(owners, r * 4 + i)

            @pl.when(mine)
            def _(i=i, r=r, slot=slot):
                pack(stats[jnp.minimum(slot, 1)], out.at[i], r * EACH + W)

        for r in range(2):
            rows = pl.ds(r * EACH, EACH)
            sends.append(pltpu.make_async_copy(out.at[i, rows], sent.at[i, rows], out_sems.at[2 * i + r]))
            sends[-1].start()
    for send in sends:
        send.wait()


def sum_kernel(tiles, out):
    total = tiles[0].astype(F32)
    for i in range(1, tiles.shape[0]):
        total += tiles[i].astype(F32)
    total = total.astype(BF)
    for i in range(out.shape[0]):
        out[i] = total


def dot(a, b):
    return jnp.dot(a, b, preferred_element_type=F32)


def root_kernel(tile, weight_in, own, first, second, third, sent, out, weight, acts, sems):
    x = lax.axis_index("x")
    copies = start_copies(
        [(weight_in.at[:, wide(x)], weight)]
        + [(part, acts.at[k]) for k, part in enumerate((own, first, second, third))],
        sems,
    )
    big_row, big_col = dims(W, W)
    identity = (big_row == big_col).astype(F32)
    grads, matrices, iterates, norms = [], [], [], []
    for r in range(2):
        grad = tile[r * EACH : r * EACH + W, :]
        old = unpack(tile, r * EACH + W)
        gram = lax.dot_general(grad, grad, (((1,), (1,)), ((), ())), preferred_element_type=F32) / W
        pack(gram, sent, r * EACH + W)
        renewed = decay_rate * old + (1.0 - decay_rate) * gram
        norm = jnp.sqrt(jnp.sum(renewed * renewed, axis=(0, 1), keepdims=True) + 1e-06)
        grads.append(grad)
        matrices.append(renewed / norm)
        norms.append(norm)
        iterates.append(None)
    for step in range(ITERS):
        for r in range(2):
            low = ((5.0 * identity - matrices[r]) / 4.0).astype(BF)
            if step == 0:
                iterates[r] = low.astype(F32)
            else:
                iterates[r] = dot(iterates[r].astype(BF), low)
            if step + 1 < ITERS:
                square = dot(low, low).astype(BF)
                fourth = dot(square, square).astype(BF)
                matrices[r] = dot(fourth, matrices[r].astype(BF))
    for copy in copies:
        copy.wait()
    news = []
    for r in range(2):
        root = (iterates[r] * lax.rsqrt(jnp.sqrt(norms[r]))).astype(BF)
        update = dot(root, grads[r]).astype(BF)
        sent[r * EACH : r * EACH + W, :] = update
        news.append((weight[r * W : (r + 1) * W, :] - step_rate * update.astype(F32)).astype(BF))
    new = jnp.concatenate(news, axis=0)
    for k in range(4):
        part = lax.dot_general(new, acts[k], (((0,), (1,)), ((), ())), preferred_element_type=F32).astype(BF)
        out[(x + (4 - k)) % 4] = part


def renewed_weight(halves, weight, new, out, sem):
    for r, (part, start) in enumerate(halves):
        rows = slice(r * W, (r + 1) * W)
        new[rows, :] = weight[rows, :] - step_rate * part[start : start + W, :].astype(F32)
    send = pltpu.make_async_copy(new, out, sem)
    send.start()
    return send


def finish_kernel(owners_in, own, third, weight_in, stats_in, weight_out, stats_out, owners, weight, stats, new, stats_new, sems, out_sems):
    x = lax.axis_index("x")
    columns = [x, (x + 1) % 4]
    copies = start_copies(
        [(owners_in, owners)]
        + [(stats_in.at[0, 0, k], stats.at[k]) for k in range(2)]
        + [(weight_in.at[:, wide(c)], weight.at[k]) for k, c in enumerate(columns)],
        sems,
    )
    sends = []
    for k, part in enumerate((own, third)):
        copies[3 + k].wait()
        halves = (part, 0), (part, EACH)
        sends.append(renewed_weight(halves, weight.at[k], new.at[k], weight_out.at[:, wide(columns[k])], out_sems.at[k]))
    for at in range(3):
        copies[at].wait()
    stats_new[...] = jnp.zeros(stats_new.shape, F32)
    for k, part in enumerate((own, third)):
        for r in range(2):
            mine, slot = mine_and_slot(owners, r * 4 + columns[k])

            @pl.when(mine)
            def _(r=r, part=part, slot=slot):
                at = jnp.minimum(slot, 1)
                stats_new[at] = decay_rate * stats[at] + (1.0 - decay_rate) * unpack(part, r * EACH + W)

    sends.append(pltpu.make_async_copy(stats_new, stats_out.at[0, 0], out_sems.at[2]))
    sends[-1].start()
    for send in sends:
        send.wait()


def last_kernel(owners_in, first, top, low, weight_in, stats_in, weight_part, stats_part, weight_out, stats_out, owners, weight, stats, new, stats_new, sems, out_sems):
    x = lax.axis_index("x")
    columns = [(x + 3) % 4, (x + 2) % 4]
    copies = start_copies(
        [(owners_in, owners)]
        + [(stats_in.at[0, 0, k], stats.at[k]) for k in range(2)]
        + [(weight_in.at[:, wide(c)], weight.at[k]) for k, c in enumerate(columns)],
        sems,
    )
    blocks = [[(first, 0), (first, EACH)], [(top, 0), (low, 0)]]
    sends = []
    for k, halves in enumerate(blocks):
        copies[3 + k].wait()
        sends.append(renewed_weight(halves, weight.at[k], new.at[k], weight_out.at[:, wide(columns[k])], out_sems.at[k]))
    for at in range(3):
        copies[at].wait()
    for k, halves in enumerate(blocks):
        for r, (part, start) in enumerate(halves):
            mine, slot = mine_and_slot(owners, r * 4 + columns[k])

            @pl.when(mine)
            def _(part=part, start=start, slot=slot):
                at = jnp.minimum(slot, 1)
                stats_new[...] = decay_rate * stats[at] + (1.0 - decay_rate) * unpack(part, start + W)
                keep = pltpu.make_async_copy(stats_new, stats_out.at[0, 0, at], out_sems.at[2])
                keep.start()
                keep.wait()

    for send in sends:
        send.wait()


def call(kernel, out, *args, specs=None, out_specs=None, scratch=(), mib=32, aliases=None):
    return pl.pallas_call(
        kernel,
        out_shape=out,
        in_specs=specs or [IN_VMEM] * len(args),
        out_specs=out_specs or jax.tree.map(lambda _: IN_VMEM, out),
        scratch_shapes=list(scratch),
        input_output_aliases=aliases or {},
        compiler_params=room(mib),
    )(*args)


def swap(x, axis):
    return lax.all_to_all(x, axis, 0, 0, tiled=True)


def turn(x, axis, by):
    n = lax.axis_size(axis)
    return lax.ppermute(x, axis, [(i, (i + by) % n) for i in range(n)])


def body(activations, cotangent, weight, stats_old, owners, next_acts):
    n_x, n_zh, n_zl, n_feat = (lax.axis_size(a) for a in ("x", "zh", "zl", "feat"))
    rows_dev, columns = weight.shape
    tokens = activations.shape[0]
    owners = owners.T
    shape = jax.ShapeDtypeStruct
    dma = pltpu.SemaphoreType.DMA
    sent = call(
        grad_kernel,
        shape((n_x, SENT, W), BF),
        owners,
        activations,
        cotangent,
        stats_old,
        specs=[IN_HBM] * 4,
        scratch=[
            pltpu.SMEM(owners.shape, jnp.int32),
            pltpu.VMEM((tokens, rows_dev), BF),
            pltpu.VMEM((tokens, columns), BF),
            pltpu.VMEM((2, W, W), F32),
            pltpu.VMEM((rows_dev, tokens), BF),
            pltpu.VMEM((n_x, SENT, W), BF),
            dma((11,)),
            dma((2 * n_x,)),
        ],
        out_specs=IN_HBM,
        mib=60,
    )
    share = SENT // n_zl
    column = call(sum_kernel, shape((1, SENT, W), BF), swap(sent, "x"))
    column, acts = lax.optimization_barrier((column, next_acts))
    acts_3 = turn(acts, "x", 3)
    tiles = swap(column.reshape(n_zl, share, W), "zl")
    tiles, acts_3 = lax.optimization_barrier((tiles, acts_3))
    part, acts = lax.optimization_barrier((call(sum_kernel, shape((n_zh, share, W), BF), tiles), acts))
    acts_2 = turn(acts, "x", 2)
    tiles, acts_2 = lax.optimization_barrier((swap(part, "zh"), acts_2))
    mine, acts = lax.optimization_barrier((call(sum_kernel, shape((n_zl, share, W), BF), tiles), acts))
    acts_1 = turn(acts, "x", 1)
    full = swap(mine, "zl").reshape(SENT, W)
    acts_1, acts_2, acts_3 = (pltpu.with_memory_space_constraint(a, pltpu.HBM) for a in (acts_1, acts_2, acts_3))
    moved, partial_next = call(
        root_kernel,
        [shape((SENT, W), BF), shape((n_x, W, tokens), BF)],
        full,
        weight,
        next_acts,
        acts_1,
        acts_2,
        acts_3,
        specs=[IN_VMEM] + [IN_HBM] * 5,
        scratch=[pltpu.VMEM((rows_dev, W), F32), pltpu.VMEM((n_x, tokens, rows_dev), BF), dma((5,))],
    )
    tiles = swap(partial_next.reshape(n_feat, columns // n_feat, tokens), "feat")
    moved_3, moved_2, moved_1 = turn(moved, "x", 3), turn(moved[:EACH], "x", 2), turn(moved, "x", 1)
    moved_2 = moved_2, turn(moved_3[EACH:], "x", 3)
    outs = [shape(weight.shape, F32), shape(stats_old.shape, F32)]
    begun = call(
        finish_kernel,
        outs,
        owners,
        moved,
        moved_3,
        weight,
        stats_old,
        specs=[IN_HBM] + [IN_VMEM] * 2 + [IN_HBM] * 2,
        out_specs=[IN_HBM, IN_HBM],
        scratch=[
            pltpu.SMEM(owners.shape, jnp.int32),
            pltpu.VMEM((2, rows_dev, W), F32),
            pltpu.VMEM((2, W, W), F32),
            pltpu.VMEM((2, rows_dev, W), F32),
            pltpu.VMEM((2, W, W), F32),
            dma((5,)),
            dma((3,)),
        ],
    )
    weight_new, stats_new = call(
        last_kernel,
        outs,
        owners,
        moved_1,
        *moved_2,
        weight,
        stats_old,
        *begun,
        specs=[IN_HBM] + [IN_VMEM] * 3 + [IN_HBM] * 4,
        out_specs=[IN_HBM, IN_HBM],
        scratch=[
            pltpu.SMEM(owners.shape, jnp.int32),
            pltpu.VMEM((2, rows_dev, W), F32),
            pltpu.VMEM((2, W, W), F32),
            pltpu.VMEM((2, rows_dev, W), F32),
            pltpu.VMEM((W, W), F32),
            dma((5,)),
            dma((3,)),
        ],
        aliases={6: 0, 7: 1},
    )
    summed = jnp.sum(tiles.astype(F32), axis=0).astype(BF)
    each = n_feat // n_x
    pairs = [
        (x * n_feat + to * each + j, to * n_feat + x * each + j)
        for x in range(n_x)
        for to in range(n_x)
        for j in range(each)
    ]
    next_out = lax.ppermute(summed, ("x", "feat"), pairs).T
    return (weight_new, stats_new, next_out)


def solution(mesh):
    torus = Mesh(mesh.devices.reshape(4, 3, 4, mesh.shape["feat"]), ("x", "zh", "zl", "feat"))
    return jax.shard_map(
        body,
        mesh=torus,
        in_specs=(
            P(DP, "feat"),
            P(DP, None),
            P("feat", None),
            P("feat", DP, None, None, None),
            P(),
            P(DP, "feat"),
        ),
        out_specs=(P("feat", None), P("feat", DP, None, None, None), P(DP, "feat")),
        check_vma=False,
    )
```

```python
import jax
import jax.numpy as jnp
from jax import lax
from jax.experimental import pallas as pl
from jax.experimental.pallas import tpu as pltpu
from jax.sharding import Mesh
from jax.sharding import PartitionSpec as P

ITERS = 6
DP = ("x", "zh", "zl")
BF = jnp.bfloat16
F32 = jnp.float32
decay_rate = 0.9
step_rate = 0.01

W = 256
H = W // 2
PACK = H + 16
EACH = W + PACK
SENT = 2 * EACH


def room(mib):
    return pltpu.CompilerParams(vmem_limit_bytes=mib * 1024 * 1024)


IN_VMEM = pl.BlockSpec(memory_space=pltpu.VMEM)
IN_HBM = pl.BlockSpec(memory_space=pltpu.HBM)


def dims(rows, cols):
    return (
        lax.broadcasted_iota(jnp.int32, (rows, cols), 0),
        lax.broadcasted_iota(jnp.int32, (rows, cols), 1),
    )


def start_copies(pairs, sems):
    copies = [pltpu.make_async_copy(a, b, sems.at[i]) for i, (a, b) in enumerate(pairs)]
    for copy in copies:
        copy.start()
    return copies


def wide(start):
    return pl.ds(pl.multiple_of(start * W, W), W)


def mine_and_slot(owners, block):
    me = (lax.axis_index("x") * 3 + lax.axis_index("zh")) * 4 + lax.axis_index("zl")
    base = lax.axis_index("feat") * 2
    mine = jnp.int32(0)
    slot = jnp.int32(0)
    for other in range(8):
        held = (owners[other % 4, base + other // 4] == me).astype(jnp.int32)
        slot += jnp.where(other < block, held, 0)
        mine += jnp.where(other == block, held, 0)
    return mine == 1, slot


def pack(old, out, start):
    row, col = dims(H, H)
    upper, lower = old[:H, :H], old[H:, H:]
    out[start : start + H, :H] = old[:H, H:].astype(BF)
    out[start : start + H, H:] = jnp.where(col >= row, upper, lower).astype(BF)
    diagonal = jnp.sum(jnp.where(row == col, lower, 0.0), axis=0, keepdims=True)
    out[start + H : start + PACK, :H] = jnp.broadcast_to(diagonal, (PACK - H, H)).astype(BF)
    out[start + H : start + PACK, H:] = jnp.zeros((PACK - H, H), BF)


def unpack(tile, start):
    row, col = dims(H, H)
    packed = tile[start : start + H, :].astype(F32)
    diagonal = tile[start + H : start + PACK, :H][:1, :].astype(F32)
    flipped = packed.T
    both, both_t = packed[:, H:], flipped[H:, :]
    upper = jnp.where(col >= row, both, both_t)
    lower = jnp.where(col < row, both, jnp.where(col > row, both_t, jnp.broadcast_to(diagonal, (H, H))))
    return jnp.concatenate(
        [
            jnp.concatenate([upper, packed[:, :H]], axis=1),
            jnp.concatenate([flipped[:H, :], lower], axis=1),
        ],
        axis=0,
    )


def grad_kernel(owners_in, acts_in, cot_in, stats_in, out, owners, acts, cot, stats, turned, sems):
    copies = start_copies(
        [(acts_in.at[:, i * H : (i + 1) * H], acts.at[:, i * H : (i + 1) * H]) for i in range(4)]
        + [(cot_in.at[:, i * W : (i + 1) * W], cot.at[:, i * W : (i + 1) * W]) for i in range(4)]
        + [(owners_in, owners)]
        + [(stats_in.at[0, 0, k], stats.at[k]) for k in range(2)],
        sems,
    )
    for r in range(2):
        for i in range(4):
            out[i, r * EACH + W : (r + 1) * EACH, :] = jnp.zeros((PACK, W), BF)
    for i in range(4):
        copies[i].wait()
        turned[i * H : (i + 1) * H, :] = acts[:, i * H : (i + 1) * H].T
    for at in (8, 9, 10):
        copies[at].wait()
    for i in range(4):
        copies[4 + i].wait()
        part = jnp.dot(turned[...], cot[:, i * W : (i + 1) * W], preferred_element_type=F32).astype(BF)
        for r in range(2):
            out[i, r * EACH : r * EACH + W, :] = part[r * W : (r + 1) * W, :]
            mine, slot = mine_and_slot(owners, r * 4 + i)

            @pl.when(mine)
            def _(i=i, r=r, slot=slot):
                pack(stats[jnp.minimum(slot, 1)], out.at[i], r * EACH + W)


def sum_kernel(tiles, out):
    total = tiles[0].astype(F32)
    for i in range(1, tiles.shape[0]):
        total += tiles[i].astype(F32)
    total = total.astype(BF)
    for i in range(out.shape[0]):
        out[i] = total


def dot(a, b):
    return jnp.dot(a, b, preferred_element_type=F32)


def root_kernel(tile, weight_in, own, first, second, third, sent, out, weight, acts, sems):
    x = lax.axis_index("x")
    copies = start_copies(
        [(weight_in.at[:, wide(x)], weight)]
        + [(part, acts.at[k]) for k, part in enumerate((own, first, second, third))],
        sems,
    )
    big_row, big_col = dims(W, W)
    identity = (big_row == big_col).astype(F32)
    grads, matrices, iterates, norms = [], [], [], []
    for r in range(2):
        grad = tile[r * EACH : r * EACH + W, :]
        old = unpack(tile, r * EACH + W)
        gram = lax.dot_general(grad, grad, (((1,), (1,)), ((), ())), preferred_element_type=F32) / W
        pack(gram, sent, r * EACH + W)
        renewed = decay_rate * old + (1.0 - decay_rate) * gram
        norm = jnp.sqrt(jnp.sum(renewed * renewed, axis=(0, 1), keepdims=True) + 1e-06)
        grads.append(grad)
        matrices.append(renewed / norm)
        norms.append(norm)
        iterates.append(None)
    for step in range(ITERS):
        for r in range(2):
            low = ((5.0 * identity - matrices[r]) / 4.0).astype(BF)
            if step == 0:
                iterates[r] = low.astype(F32)
            else:
                iterates[r] = dot(iterates[r].astype(BF), low)
            if step + 1 < ITERS:
                square = dot(low, low).astype(BF)
                fourth = dot(square, square).astype(BF)
                matrices[r] = dot(fourth, matrices[r].astype(BF))
    for copy in copies:
        copy.wait()
    news = []
    for r in range(2):
        root = (iterates[r] * lax.rsqrt(jnp.sqrt(norms[r]))).astype(BF)
        update = dot(root, grads[r]).astype(BF)
        sent[r * EACH : r * EACH + W, :] = update
        news.append((weight[r * W : (r + 1) * W, :] - step_rate * update.astype(F32)).astype(BF))
    new = jnp.concatenate(news, axis=0)
    for k in range(4):
        part = lax.dot_general(new, acts[k], (((0,), (1,)), ((), ())), preferred_element_type=F32).astype(BF)
        out[(x + (4 - k)) % 4] = part


def renewed_weight(halves, weight, new, out, sem):
    for r, (part, start) in enumerate(halves):
        rows = slice(r * W, (r + 1) * W)
        new[rows, :] = weight[rows, :] - step_rate * part[start : start + W, :].astype(F32)
    send = pltpu.make_async_copy(new, out, sem)
    send.start()
    return send


def finish_kernel(owners_in, own, weight_in, stats_in, weight_out, stats_out, owners, weight, stats, new, stats_new, sems, out_sems):
    x = lax.axis_index("x")
    copies = start_copies(
        [(owners_in, owners)]
        + [(stats_in.at[0, 0, k], stats.at[k]) for k in range(2)]
        + [(weight_in.at[:, wide(x)], weight)],
        sems,
    )
    copies[3].wait()
    sends = [renewed_weight([(own, 0), (own, EACH)], weight, new, weight_out.at[:, wide(x)], out_sems.at[0])]
    for at in range(3):
        copies[at].wait()
    stats_new[...] = jnp.zeros(stats_new.shape, F32)
    for r in range(2):
        mine, slot = mine_and_slot(owners, r * 4 + x)

        @pl.when(mine)
        def _(r=r, slot=slot):
            at = jnp.minimum(slot, 1)
            stats_new[at] = decay_rate * stats[at] + (1.0 - decay_rate) * unpack(own, r * EACH + W)

    sends.append(pltpu.make_async_copy(stats_new, stats_out.at[0, 0], out_sems.at[1]))
    sends[-1].start()
    for send in sends:
        send.wait()


def last_kernel(owners_in, third, first, top, low, weight_in, stats_in, weight_part, stats_part, weight_out, stats_out, owners, weight, stats, new, stats_new, sems, out_sems):
    x = lax.axis_index("x")
    columns = [(x + 1) % 4, (x + 3) % 4, (x + 2) % 4]
    copies = start_copies(
        [(owners_in, owners)]
        + [(stats_in.at[0, 0, k], stats.at[k]) for k in range(2)]
        + [(weight_in.at[:, wide(c)], weight.at[k]) for k, c in enumerate(columns)],
        sems,
    )
    blocks = [[(third, 0), (third, EACH)], [(first, 0), (first, EACH)], [(top, 0), (low, 0)]]
    sends = []
    for k, halves in enumerate(blocks):
        copies[3 + k].wait()
        sends.append(renewed_weight(halves, weight.at[k], new.at[k], weight_out.at[:, wide(columns[k])], out_sems.at[k]))
    for at in range(3):
        copies[at].wait()
    for k, halves in enumerate(blocks):
        for r, (part, start) in enumerate(halves):
            mine, slot = mine_and_slot(owners, r * 4 + columns[k])

            @pl.when(mine)
            def _(part=part, start=start, slot=slot):
                at = jnp.minimum(slot, 1)
                stats_new[...] = decay_rate * stats[at] + (1.0 - decay_rate) * unpack(part, start + W)
                keep = pltpu.make_async_copy(stats_new, stats_out.at[0, 0, at], out_sems.at[3])
                keep.start()
                keep.wait()

    for send in sends:
        send.wait()


def call(kernel, out, *args, specs=None, out_specs=None, scratch=(), mib=32, aliases=None):
    return pl.pallas_call(
        kernel,
        out_shape=out,
        in_specs=specs or [IN_VMEM] * len(args),
        out_specs=out_specs or jax.tree.map(lambda _: IN_VMEM, out),
        scratch_shapes=list(scratch),
        input_output_aliases=aliases or {},
        compiler_params=room(mib),
    )(*args)


def swap(x, axis):
    return lax.all_to_all(x, axis, 0, 0, tiled=True)


def turn(x, axis, by):
    n = lax.axis_size(axis)
    return lax.ppermute(x, axis, [(i, (i + by) % n) for i in range(n)])


def body(activations, cotangent, weight, stats_old, owners, next_acts):
    n_x, n_zh, n_zl, n_feat = (lax.axis_size(a) for a in ("x", "zh", "zl", "feat"))
    rows_dev, columns = weight.shape
    tokens = activations.shape[0]
    owners = owners.T
    shape = jax.ShapeDtypeStruct
    dma = pltpu.SemaphoreType.DMA
    sent = call(
        grad_kernel,
        shape((n_x, SENT, W), BF),
        *[pltpu.with_memory_space_constraint(a, pltpu.HBM) for a in (owners, activations, cotangent, stats_old)],
        specs=[IN_HBM] * 4,
        scratch=[
            pltpu.SMEM(owners.shape, jnp.int32),
            pltpu.VMEM((tokens, rows_dev), BF),
            pltpu.VMEM((tokens, columns), BF),
            pltpu.VMEM((2, W, W), F32),
            pltpu.VMEM((rows_dev, tokens), BF),
            dma((11,)),
        ],
    )
    share = SENT // n_zl
    column = call(sum_kernel, shape((1, SENT, W), BF), swap(sent, "x"))
    column, acts = lax.optimization_barrier((column, next_acts))
    acts_3 = turn(acts, "x", 3)
    tiles = swap(column.reshape(n_zl, share, W), "zl")
    tiles, acts_3 = lax.optimization_barrier((tiles, acts_3))
    part, acts = lax.optimization_barrier((call(sum_kernel, shape((n_zh, share, W), BF), tiles), acts))
    acts_2 = turn(acts, "x", 2)
    tiles, acts_2 = lax.optimization_barrier((swap(part, "zh"), acts_2))
    mine, acts = lax.optimization_barrier((call(sum_kernel, shape((n_zl, share, W), BF), tiles), acts))
    acts_1 = turn(acts, "x", 1)
    full = swap(mine, "zl").reshape(SENT, W)
    acts_1, acts_2, acts_3 = (pltpu.with_memory_space_constraint(a, pltpu.HBM) for a in (acts_1, acts_2, acts_3))
    moved, partial_next = call(
        root_kernel,
        [shape((SENT, W), BF), shape((n_x, W, tokens), BF)],
        full,
        weight,
        pltpu.with_memory_space_constraint(next_acts, pltpu.HBM),
        acts_1,
        acts_2,
        acts_3,
        specs=[IN_VMEM] + [IN_HBM] * 5,
        scratch=[pltpu.VMEM((rows_dev, W), F32), pltpu.VMEM((n_x, tokens, rows_dev), BF), dma((5,))],
        mib=32,
    )
    tiles = swap(partial_next.reshape(n_feat, columns // n_feat, tokens), "feat")
    moved_3, moved_2, moved_1 = turn(moved, "x", 3), turn(moved[:EACH], "x", 2), turn(moved, "x", 1)
    outs = [shape(weight.shape, F32), shape(stats_old.shape, F32)]
    begun = list(call(
        finish_kernel,
        outs,
        owners,
        moved,
        weight,
        stats_old,
        specs=[IN_HBM, IN_VMEM, IN_HBM, IN_HBM],
        out_specs=[IN_HBM, IN_HBM],
        scratch=[
            pltpu.SMEM(owners.shape, jnp.int32),
            pltpu.VMEM((rows_dev, W), F32),
            pltpu.VMEM((2, W, W), F32),
            pltpu.VMEM((rows_dev, W), F32),
            pltpu.VMEM((2, W, W), F32),
            dma((4,)),
            dma((2,)),
        ],
    ))
    begun[0], begun[1], handed = lax.optimization_barrier((*begun, moved_3))
    moved_2 = moved_2, turn(handed[EACH:], "x", 3)
    weight_new, stats_new = call(
        last_kernel,
        outs,
        owners,
        moved_3,
        moved_1,
        *moved_2,
        weight,
        stats_old,
        *begun,
        specs=[IN_HBM] + [IN_VMEM] * 4 + [IN_HBM] * 4,
        out_specs=[IN_HBM, IN_HBM],
        scratch=[
            pltpu.SMEM(owners.shape, jnp.int32),
            pltpu.VMEM((3, rows_dev, W), F32),
            pltpu.VMEM((2, W, W), F32),
            pltpu.VMEM((3, rows_dev, W), F32),
            pltpu.VMEM((W, W), F32),
            dma((6,)),
            dma((4,)),
        ],
        aliases={7: 0, 8: 1},
    )
    summed = jnp.sum(tiles.astype(F32), axis=0).astype(BF)
    each = n_feat // n_x
    pairs = [
        (x * n_feat + to * each + j, to * n_feat + x * each + j)
        for x in range(n_x)
        for to in range(n_x)
        for j in range(each)
    ]
    next_out = lax.ppermute(summed, ("x", "feat"), pairs).T
    return (weight_new, stats_new, next_out)


def solution(mesh):
    torus = Mesh(mesh.devices.reshape(4, 3, 4, mesh.shape["feat"]), ("x", "zh", "zl", "feat"))
    return jax.shard_map(
        body,
        mesh=torus,
        in_specs=(
            P(DP, "feat"),
            P(DP, None),
            P("feat", None),
            P("feat", DP, None, None, None),
            P(),
            P(DP, "feat"),
        ),
        out_specs=(P("feat", None), P("feat", DP, None, None, None), P(DP, "feat")),
        check_vma=False,
    )
```

```python
import jax
import jax.numpy as jnp
from jax import lax
from jax.experimental import pallas as pl
from jax.experimental.pallas import tpu as pltpu
from jax.sharding import Mesh
from jax.sharding import PartitionSpec as P

ITERS = 6
DP = ("x", "zh", "zl")
BF = jnp.bfloat16
F32 = jnp.float32
decay_rate = 0.9
step_rate = 0.01

W = 256
H = W // 2
PACK = H + 16
EACH = W + PACK
SENT = 2 * EACH


def room(mib):
    return pltpu.CompilerParams(vmem_limit_bytes=mib * 1024 * 1024)


IN_VMEM = pl.BlockSpec(memory_space=pltpu.VMEM)
IN_HBM = pl.BlockSpec(memory_space=pltpu.HBM)


def dims(rows, cols):
    return (
        lax.broadcasted_iota(jnp.int32, (rows, cols), 0),
        lax.broadcasted_iota(jnp.int32, (rows, cols), 1),
    )


def start_copies(pairs, sems):
    copies = [pltpu.make_async_copy(a, b, sems.at[i]) for i, (a, b) in enumerate(pairs)]
    for copy in copies:
        copy.start()
    return copies


def wide(start):
    return pl.ds(pl.multiple_of(start * W, W), W)


def mine_and_slot(owners, block):
    me = (lax.axis_index("x") * 3 + lax.axis_index("zh")) * 4 + lax.axis_index("zl")
    base = lax.axis_index("feat") * 2
    mine = jnp.int32(0)
    slot = jnp.int32(0)
    for other in range(8):
        held = (owners[other % 4, base + other // 4] == me).astype(jnp.int32)
        slot += jnp.where(other < block, held, 0)
        mine += jnp.where(other == block, held, 0)
    return mine == 1, slot


def pack(old, out, start):
    row, col = dims(H, H)
    upper, lower = old[:H, :H], old[H:, H:]
    out[start : start + H, :H] = old[:H, H:].astype(BF)
    out[start : start + H, H:] = jnp.where(col >= row, upper, lower).astype(BF)
    diagonal = jnp.sum(jnp.where(row == col, lower, 0.0), axis=0, keepdims=True)
    out[start + H : start + PACK, :H] = jnp.broadcast_to(diagonal, (PACK - H, H)).astype(BF)
    out[start + H : start + PACK, H:] = jnp.zeros((PACK - H, H), BF)


def unpack(tile, start):
    row, col = dims(H, H)
    packed = tile[start : start + H, :].astype(F32)
    diagonal = tile[start + H : start + PACK, :H][:1, :].astype(F32)
    flipped = packed.T
    both, both_t = packed[:, H:], flipped[H:, :]
    upper = jnp.where(col >= row, both, both_t)
    lower = jnp.where(col < row, both, jnp.where(col > row, both_t, jnp.broadcast_to(diagonal, (H, H))))
    return jnp.concatenate(
        [
            jnp.concatenate([upper, packed[:, :H]], axis=1),
            jnp.concatenate([flipped[:H, :], lower], axis=1),
        ],
        axis=0,
    )


def grad_kernel(owners_in, acts_in, cot_in, stats_in, out, owners, acts, cot, stats, turned, sems):
    copies = start_copies(
        [(acts_in.at[:, i * H : (i + 1) * H], acts.at[:, i * H : (i + 1) * H]) for i in range(4)]
        + [(cot_in.at[:, i * W : (i + 1) * W], cot.at[:, i * W : (i + 1) * W]) for i in range(4)]
        + [(owners_in, owners)]
        + [(stats_in.at[0, 0, k], stats.at[k]) for k in range(2)],
        sems,
    )
    for r in range(2):
        for i in range(4):
            out[i, r * EACH + W : (r + 1) * EACH, :] = jnp.zeros((PACK, W), BF)
    for i in range(4):
        copies[i].wait()
        turned[i * H : (i + 1) * H, :] = acts[:, i * H : (i + 1) * H].T
    for at in (8, 9, 10):
        copies[at].wait()
    for i in range(4):
        copies[4 + i].wait()
        part = jnp.dot(turned[...], cot[:, i * W : (i + 1) * W], preferred_element_type=F32).astype(BF)
        for r in range(2):
            out[i, r * EACH : r * EACH + W, :] = part[r * W : (r + 1) * W, :]
            mine, slot = mine_and_slot(owners, r * 4 + i)

            @pl.when(mine)
            def _(i=i, r=r, slot=slot):
                pack(stats[jnp.minimum(slot, 1)], out.at[i], r * EACH + W)


def sum_rows_kernel(tiles, out, total, sems):
    sends = []
    step = tiles.shape[1] // sems.shape[0]
    for piece in range(sems.shape[0]):
        rows = slice(piece * step, (piece + 1) * step)
        part = tiles[0, rows, :].astype(F32)
        for i in range(1, tiles.shape[0]):
            part += tiles[i, rows, :].astype(F32)
        total[rows, :] = part.astype(BF)
        sends.append(pltpu.make_async_copy(total.at[rows], out.at[rows], sems.at[piece]))
        sends[-1].start()
    for send in sends:
        send.wait()


def sum_kernel(tiles, out, total, sems):
    part = tiles[0].astype(F32)
    for i in range(1, tiles.shape[0]):
        part += tiles[i].astype(F32)
    total[...] = part.astype(BF)
    sends = start_copies([(total, out.at[i]) for i in range(out.shape[0])], sems)
    for send in sends:
        send.wait()


def gather_sum_kernel(tiles_in, out, tiles, sems):
    step = tiles.shape[0] // sems.shape[0]
    pieces = [pl.ds(i * step, step) for i in range(sems.shape[0])]
    copies = start_copies([(tiles_in.at[piece], tiles.at[piece]) for piece in pieces], sems)
    total = jnp.zeros(tiles.shape[1:], F32)
    for i in range(tiles.shape[0]):
        if i % step == 0:
            copies[i // step].wait()
        total += tiles[i].astype(F32)
    out[...] = total.astype(BF)


def dot(a, b):
    return jnp.dot(a, b, preferred_element_type=F32)


def root_kernel(tile, weight_in, own, first, second, third, sent, out, weight, acts, sems):
    x = lax.axis_index("x")
    copies = start_copies(
        [(weight_in.at[:, wide(x)], weight)]
        + [(part, acts.at[k]) for k, part in enumerate((own, first, second, third))],
        sems,
    )
    big_row, big_col = dims(W, W)
    identity = (big_row == big_col).astype(F32)
    grads, matrices, iterates, norms = [], [], [], []
    for r in range(2):
        grad = tile[r * EACH : r * EACH + W, :]
        old = unpack(tile, r * EACH + W)
        gram = lax.dot_general(grad, grad, (((1,), (1,)), ((), ())), preferred_element_type=F32) / W
        pack(gram, sent, r * EACH + W)
        renewed = decay_rate * old + (1.0 - decay_rate) * gram
        norm = jnp.sqrt(jnp.sum(renewed * renewed, axis=(0, 1), keepdims=True) + 1e-06)
        grads.append(grad)
        matrices.append(renewed / norm)
        norms.append(norm)
        iterates.append(None)
    for step in range(ITERS):
        for r in range(2):
            low = ((5.0 * identity - matrices[r]) / 4.0).astype(BF)
            if step == 0:
                iterates[r] = low.astype(F32)
            else:
                iterates[r] = dot(iterates[r].astype(BF), low)
            if step + 1 < ITERS:
                square = dot(low, low).astype(BF)
                fourth = dot(square, square).astype(BF)
                matrices[r] = dot(fourth, matrices[r].astype(BF))
    for copy in copies:
        copy.wait()
    news = []
    for r in range(2):
        root = (iterates[r] * lax.rsqrt(jnp.sqrt(norms[r]))).astype(BF)
        update = dot(root, grads[r]).astype(BF)
        sent[r * EACH : r * EACH + W, :] = update
        news.append((weight[r * W : (r + 1) * W, :] - step_rate * update.astype(F32)).astype(BF))
    new = jnp.concatenate(news, axis=0)
    for k in range(4):
        part = lax.dot_general(new, acts[k], (((0,), (1,)), ((), ())), preferred_element_type=F32).astype(BF)
        out[(x + (4 - k)) % 4] = part


def renewed_weight(halves, weight, new, out, sem):
    for r, (part, start) in enumerate(halves):
        rows = slice(r * W, (r + 1) * W)
        new[rows, :] = weight[rows, :] - step_rate * part[start : start + W, :].astype(F32)
    send = pltpu.make_async_copy(new, out, sem)
    send.start()
    return send


def finish_kernel(owners_in, own, weight_in, stats_in, weight_out, stats_out, owners, weight, stats, new, stats_new, sems, out_sems):
    x = lax.axis_index("x")
    copies = start_copies(
        [(owners_in, owners)]
        + [(stats_in.at[0, 0, k], stats.at[k]) for k in range(2)]
        + [(weight_in.at[:, wide(x)], weight)],
        sems,
    )
    copies[3].wait()
    sends = [renewed_weight([(own, 0), (own, EACH)], weight, new, weight_out.at[:, wide(x)], out_sems.at[0])]
    for at in range(3):
        copies[at].wait()
    stats_new[...] = jnp.zeros(stats_new.shape, F32)
    for r in range(2):
        mine, slot = mine_and_slot(owners, r * 4 + x)

        @pl.when(mine)
        def _(r=r, slot=slot):
            at = jnp.minimum(slot, 1)
            stats_new[at] = decay_rate * stats[at] + (1.0 - decay_rate) * unpack(own, r * EACH + W)

    sends.append(pltpu.make_async_copy(stats_new, stats_out.at[0, 0], out_sems.at[1]))
    sends[-1].start()
    for send in sends:
        send.wait()


def last_kernel(owners_in, third, first, top, low, weight_in, stats_in, weight_part, stats_part, weight_out, stats_out, owners, weight, stats, new, stats_new, sems, out_sems):
    x = lax.axis_index("x")
    columns = [(x + 1) % 4, (x + 3) % 4, (x + 2) % 4]
    copies = start_copies(
        [(owners_in, owners)]
        + [(stats_in.at[0, 0, k], stats.at[k]) for k in range(2)]
        + [(weight_in.at[:, wide(c)], weight.at[k]) for k, c in enumerate(columns)],
        sems,
    )
    blocks = [[(third, 0), (third, EACH)], [(first, 0), (first, EACH)], [(top, 0), (low, 0)]]
    sends = []
    for k, halves in enumerate(blocks):
        copies[3 + k].wait()
        sends.append(renewed_weight(halves, weight.at[k], new.at[k], weight_out.at[:, wide(columns[k])], out_sems.at[k]))
    for at in range(3):
        copies[at].wait()
    for k, halves in enumerate(blocks):
        for r, (part, start) in enumerate(halves):
            mine, slot = mine_and_slot(owners, r * 4 + columns[k])

            @pl.when(mine)
            def _(part=part, start=start, slot=slot):
                at = jnp.minimum(slot, 1)
                stats_new[...] = decay_rate * stats[at] + (1.0 - decay_rate) * unpack(part, start + W)
                keep = pltpu.make_async_copy(stats_new, stats_out.at[0, 0, at], out_sems.at[3])
                keep.start()
                keep.wait()

    for send in sends:
        send.wait()


def call(kernel, out, *args, specs=None, out_specs=None, scratch=(), mib=32, aliases=None):
    return pl.pallas_call(
        kernel,
        out_shape=out,
        in_specs=specs or [IN_VMEM] * len(args),
        out_specs=out_specs or jax.tree.map(lambda _: IN_VMEM, out),
        scratch_shapes=list(scratch),
        input_output_aliases=aliases or {},
        compiler_params=room(mib),
    )(*args)


def swap(x, axis):
    return lax.all_to_all(x, axis, 0, 0, tiled=True)


def turn(x, axis, by):
    n = lax.axis_size(axis)
    return lax.ppermute(x, axis, [(i, (i + by) % n) for i in range(n)])


def body(activations, cotangent, weight, stats_old, owners, next_acts):
    n_x, n_zh, n_zl, n_feat = (lax.axis_size(a) for a in ("x", "zh", "zl", "feat"))
    rows_dev, columns = weight.shape
    tokens = activations.shape[0]
    owners = owners.T
    shape = jax.ShapeDtypeStruct
    dma = pltpu.SemaphoreType.DMA
    sent = call(
        grad_kernel,
        shape((n_x, SENT, W), BF),
        *[pltpu.with_memory_space_constraint(a, pltpu.HBM) for a in (owners, activations, cotangent, stats_old)],
        specs=[IN_HBM] * 4,
        scratch=[
            pltpu.SMEM(owners.shape, jnp.int32),
            pltpu.VMEM((tokens, rows_dev), BF),
            pltpu.VMEM((tokens, columns), BF),
            pltpu.VMEM((2, W, W), F32),
            pltpu.VMEM((rows_dev, tokens), BF),
            dma((11,)),
        ],
    )
    share = SENT // n_zl

    def copies_of_sum(count, tiles):
        return call(
            sum_kernel,
            shape((count, share, W), BF),
            tiles,
            out_specs=IN_HBM,
            scratch=[pltpu.VMEM((share, W), BF), dma((count,))],
        )

    column = call(
        sum_rows_kernel,
        shape((SENT, W), BF),
        swap(sent, "x"),
        out_specs=IN_HBM,
        scratch=[pltpu.VMEM((SENT, W), BF), dma((5,))],
    )
    column, acts = lax.optimization_barrier((column, next_acts))
    acts_3 = turn(acts, "x", 3)
    tiles = swap(column.reshape(n_zl, share, W), "zl")
    tiles, acts_3 = lax.optimization_barrier((tiles, acts_3))
    part, acts = lax.optimization_barrier((copies_of_sum(n_zh, tiles), acts))
    acts_2 = turn(acts, "x", 2)
    tiles, acts_2 = lax.optimization_barrier((swap(part, "zh"), acts_2))
    mine, acts = lax.optimization_barrier((copies_of_sum(n_zl, tiles), acts))
    acts_1 = turn(acts, "x", 1)
    full = swap(mine, "zl").reshape(SENT, W)
    acts_1, acts_2, acts_3 = (pltpu.with_memory_space_constraint(a, pltpu.HBM) for a in (acts_1, acts_2, acts_3))
    moved, partial_next = call(
        root_kernel,
        [shape((SENT, W), BF), shape((n_x, W, tokens), BF)],
        full,
        weight,
        pltpu.with_memory_space_constraint(next_acts, pltpu.HBM),
        acts_1,
        acts_2,
        acts_3,
        specs=[IN_VMEM] + [IN_HBM] * 5,
        scratch=[pltpu.VMEM((rows_dev, W), F32), pltpu.VMEM((n_x, tokens, rows_dev), BF), dma((5,))],
        mib=32,
    )
    tiles = swap(partial_next.reshape(n_feat, columns // n_feat, tokens), "feat")
    moved_3, moved_2, moved_1 = turn(moved, "x", 3), turn(moved[:EACH], "x", 2), turn(moved, "x", 1)
    outs = [shape(weight.shape, F32), shape(stats_old.shape, F32)]
    begun = list(call(
        finish_kernel,
        outs,
        owners,
        moved,
        weight,
        stats_old,
        specs=[IN_HBM, IN_VMEM, IN_HBM, IN_HBM],
        out_specs=[IN_HBM, IN_HBM],
        scratch=[
            pltpu.SMEM(owners.shape, jnp.int32),
            pltpu.VMEM((rows_dev, W), F32),
            pltpu.VMEM((2, W, W), F32),
            pltpu.VMEM((rows_dev, W), F32),
            pltpu.VMEM((2, W, W), F32),
            dma((4,)),
            dma((2,)),
        ],
    ))
    begun[0], begun[1], handed = lax.optimization_barrier((*begun, moved_3))
    moved_2 = moved_2, turn(handed[EACH:], "x", 3)
    weight_new, stats_new = call(
        last_kernel,
        outs,
        owners,
        moved_3,
        moved_1,
        *moved_2,
        weight,
        stats_old,
        *begun,
        specs=[IN_HBM] + [IN_VMEM] * 4 + [IN_HBM] * 4,
        out_specs=[IN_HBM, IN_HBM],
        scratch=[
            pltpu.SMEM(owners.shape, jnp.int32),
            pltpu.VMEM((3, rows_dev, W), F32),
            pltpu.VMEM((2, W, W), F32),
            pltpu.VMEM((3, rows_dev, W), F32),
            pltpu.VMEM((W, W), F32),
            dma((6,)),
            dma((4,)),
        ],
        aliases={7: 0, 8: 1},
    )
    summed = call(
        gather_sum_kernel,
        shape(tiles.shape[1:], BF),
        pltpu.with_memory_space_constraint(tiles, pltpu.HBM),
        specs=[IN_HBM],
        scratch=[pltpu.VMEM(tiles.shape, BF), dma((8,))],
    )
    each = n_feat // n_x
    pairs = [
        (x * n_feat + to * each + j, to * n_feat + x * each + j)
        for x in range(n_x)
        for to in range(n_x)
        for j in range(each)
    ]
    next_out = lax.ppermute(summed, ("x", "feat"), pairs).T
    return (weight_new, stats_new, next_out)


def solution(mesh):
    torus = Mesh(mesh.devices.reshape(4, 3, 4, mesh.shape["feat"]), ("x", "zh", "zl", "feat"))
    return jax.shard_map(
        body,
        mesh=torus,
        in_specs=(
            P(DP, "feat"),
            P(DP, None),
            P("feat", None),
            P("feat", DP, None, None, None),
            P(),
            P(DP, "feat"),
        ),
        out_specs=(P("feat", None), P("feat", DP, None, None, None), P(DP, "feat")),
        check_vma=False,
    )
```

```python
import jax
import jax.numpy as jnp
from jax import lax
from jax.experimental import pallas as pl
from jax.experimental.pallas import tpu as pltpu
from jax.sharding import Mesh
from jax.sharding import PartitionSpec as P

ITERS = 6
DP = ("x", "zh", "zl")
BF = jnp.bfloat16
F32 = jnp.float32
decay_rate = 0.9
step_rate = 0.01

W = 256
H = W // 2
PACK = H + 16
EACH = W + PACK
SENT = 2 * EACH


def room(mib):
    return pltpu.CompilerParams(vmem_limit_bytes=mib * 1024 * 1024)


IN_VMEM = pl.BlockSpec(memory_space=pltpu.VMEM)
IN_HBM = pl.BlockSpec(memory_space=pltpu.HBM)


def dims(rows, cols):
    return (
        lax.broadcasted_iota(jnp.int32, (rows, cols), 0),
        lax.broadcasted_iota(jnp.int32, (rows, cols), 1),
    )


def start_copies(pairs, sems):
    copies = [pltpu.make_async_copy(a, b, sems.at[i]) for i, (a, b) in enumerate(pairs)]
    for copy in copies:
        copy.start()
    return copies


def wide(start):
    return pl.ds(pl.multiple_of(start * W, W), W)


def mine_and_slot(owners, block):
    me = (lax.axis_index("x") * 3 + lax.axis_index("zh")) * 4 + lax.axis_index("zl")
    base = lax.axis_index("feat") * 2
    mine = jnp.int32(0)
    slot = jnp.int32(0)
    for other in range(8):
        held = (owners[other % 4, base + other // 4] == me).astype(jnp.int32)
        slot += jnp.where(other < block, held, 0)
        mine += jnp.where(other == block, held, 0)
    return mine == 1, slot


def pack(old, out, start):
    row, col = dims(H, H)
    upper, lower = old[:H, :H], old[H:, H:]
    out[start : start + H, :H] = old[:H, H:].astype(BF)
    out[start : start + H, H:] = jnp.where(col >= row, upper, lower).astype(BF)
    diagonal = jnp.sum(jnp.where(row == col, lower, 0.0), axis=0, keepdims=True)
    out[start + H : start + PACK, :H] = jnp.broadcast_to(diagonal, (PACK - H, H)).astype(BF)
    out[start + H : start + PACK, H:] = jnp.zeros((PACK - H, H), BF)


def unpack(tile, start):
    row, col = dims(H, H)
    packed = tile[start : start + H, :].astype(F32)
    diagonal = tile[start + H : start + PACK, :H][:1, :].astype(F32)
    flipped = packed.T
    both, both_t = packed[:, H:], flipped[H:, :]
    upper = jnp.where(col >= row, both, both_t)
    lower = jnp.where(col < row, both, jnp.where(col > row, both_t, jnp.broadcast_to(diagonal, (H, H))))
    return jnp.concatenate(
        [
            jnp.concatenate([upper, packed[:, :H]], axis=1),
            jnp.concatenate([flipped[:H, :], lower], axis=1),
        ],
        axis=0,
    )


def grad_kernel(owners_in, acts_in, cot_in, stats_in, out, owners, acts, cot, stats, turned, sems):
    copies = start_copies(
        [(acts_in.at[:, i * H : (i + 1) * H], acts.at[:, i * H : (i + 1) * H]) for i in range(4)]
        + [(cot_in.at[:, i * W : (i + 1) * W], cot.at[:, i * W : (i + 1) * W]) for i in range(4)]
        + [(owners_in, owners)]
        + [(stats_in.at[0, 0, k], stats.at[k]) for k in range(2)],
        sems,
    )
    for r in range(2):
        for i in range(4):
            out[i, r * EACH + W : (r + 1) * EACH, :] = jnp.zeros((PACK, W), BF)
    for i in range(4):
        copies[i].wait()
        turned[i * H : (i + 1) * H, :] = acts[:, i * H : (i + 1) * H].T
    for at in (8, 9, 10):
        copies[at].wait()
    for i in range(4):
        copies[4 + i].wait()
        part = jnp.dot(turned[...], cot[:, i * W : (i + 1) * W], preferred_element_type=F32).astype(BF)
        for r in range(2):
            out[i, r * EACH : r * EACH + W, :] = part[r * W : (r + 1) * W, :]
            mine, slot = mine_and_slot(owners, r * 4 + i)

            @pl.when(mine)
            def _(i=i, r=r, slot=slot):
                pack(stats[jnp.minimum(slot, 1)], out.at[i], r * EACH + W)


def sum_kernel(tiles, out):
    total = tiles[0].astype(F32)
    for i in range(1, tiles.shape[0]):
        total += tiles[i].astype(F32)
    total = total.astype(BF)
    for i in range(out.shape[0]):
        out[i] = total


def dot(a, b):
    return jnp.dot(a, b, preferred_element_type=F32)


def root_kernel(tile, weight_in, own, first, second, third, sent, out, weight, acts, sems):
    x = lax.axis_index("x")
    copies = start_copies(
        [(weight_in.at[:, wide(x)], weight)]
        + [(part, acts.at[k]) for k, part in enumerate((own, first, second, third))],
        sems,
    )
    big_row, big_col = dims(W, W)
    identity = (big_row == big_col).astype(F32)
    grads, matrices, iterates, norms = [], [], [], []
    for r in range(2):
        grad = tile[r * EACH : r * EACH + W, :]
        old = unpack(tile, r * EACH + W)
        gram = lax.dot_general(grad, grad, (((1,), (1,)), ((), ())), preferred_element_type=F32) / W
        pack(gram, sent, r * EACH + W)
        renewed = decay_rate * old + (1.0 - decay_rate) * gram
        norm = jnp.sqrt(jnp.sum(renewed * renewed, axis=(0, 1), keepdims=True) + 1e-06)
        grads.append(grad)
        matrices.append(renewed / norm)
        norms.append(norm)
        iterates.append(None)
    for step in range(ITERS):
        lows = [((5.0 * identity - matrix) / 4.0).astype(BF) for matrix in matrices]
        if step + 1 < ITERS:
            squares = [dot(low, low).astype(BF) for low in lows]
        if step == 0:
            iterates = [low.astype(F32) for low in lows]
        else:
            iterates = [dot(iterate.astype(BF), low) for iterate, low in zip(iterates, lows)]
        if step + 1 < ITERS:
            fourths = [dot(square, square).astype(BF) for square in squares]
            matrices = [dot(fourth, matrix.astype(BF)) for fourth, matrix in zip(fourths, matrices)]
    for copy in copies:
        copy.wait()
    news = []
    for r in range(2):
        root = (iterates[r] * lax.rsqrt(jnp.sqrt(norms[r]))).astype(BF)
        update = dot(root, grads[r]).astype(BF)
        sent[r * EACH : r * EACH + W, :] = update
        news.append((weight[r * W : (r + 1) * W, :] - step_rate * update.astype(F32)).astype(BF))
    new = jnp.concatenate(news, axis=0)
    for k in range(4):
        part = lax.dot_general(new, acts[k], (((0,), (1,)), ((), ())), preferred_element_type=F32).astype(BF)
        out[(x + (4 - k)) % 4] = part


def renewed_weight(halves, weight, new, out, sem):
    for r, (part, start) in enumerate(halves):
        rows = slice(r * W, (r + 1) * W)
        new[rows, :] = weight[rows, :] - step_rate * part[start : start + W, :].astype(F32)
    send = pltpu.make_async_copy(new, out, sem)
    send.start()
    return send


def finish_kernel(owners_in, own, weight_in, stats_in, weight_out, stats_out, owners, weight, stats, new, stats_new, sems, out_sems):
    x = lax.axis_index("x")
    copies = start_copies(
        [(owners_in, owners)]
        + [(stats_in.at[0, 0, k], stats.at[k]) for k in range(2)]
        + [(weight_in.at[:, wide(x)], weight)],
        sems,
    )
    copies[3].wait()
    sends = [renewed_weight([(own, 0), (own, EACH)], weight, new, weight_out.at[:, wide(x)], out_sems.at[0])]
    for at in range(3):
        copies[at].wait()
    stats_new[...] = jnp.zeros(stats_new.shape, F32)
    for r in range(2):
        mine, slot = mine_and_slot(owners, r * 4 + x)

        @pl.when(mine)
        def _(r=r, slot=slot):
            at = jnp.minimum(slot, 1)
            stats_new[at] = decay_rate * stats[at] + (1.0 - decay_rate) * unpack(own, r * EACH + W)

    sends.append(pltpu.make_async_copy(stats_new, stats_out.at[0, 0], out_sems.at[1]))
    sends[-1].start()
    for send in sends:
        send.wait()


def last_kernel(owners_in, third, first, top, low, weight_in, stats_in, weight_part, stats_part, weight_out, stats_out, owners, weight, stats, new, stats_new, sems, out_sems):
    x = lax.axis_index("x")
    columns = [(x + 1) % 4, (x + 3) % 4, (x + 2) % 4]
    copies = start_copies(
        [(owners_in, owners)]
        + [(stats_in.at[0, 0, k], stats.at[k]) for k in range(2)]
        + [(weight_in.at[:, wide(c)], weight.at[k]) for k, c in enumerate(columns)],
        sems,
    )
    blocks = [[(third, 0), (third, EACH)], [(first, 0), (first, EACH)], [(top, 0), (low, 0)]]
    sends = []
    for k, halves in enumerate(blocks):
        copies[3 + k].wait()
        sends.append(renewed_weight(halves, weight.at[k], new.at[k], weight_out.at[:, wide(columns[k])], out_sems.at[k]))
    for at in range(3):
        copies[at].wait()
    for k, halves in enumerate(blocks):
        for r, (part, start) in enumerate(halves):
            mine, slot = mine_and_slot(owners, r * 4 + columns[k])

            @pl.when(mine)
            def _(part=part, start=start, slot=slot):
                at = jnp.minimum(slot, 1)
                stats_new[...] = decay_rate * stats[at] + (1.0 - decay_rate) * unpack(part, start + W)
                keep = pltpu.make_async_copy(stats_new, stats_out.at[0, 0, at], out_sems.at[3])
                keep.start()
                keep.wait()

    for send in sends:
        send.wait()


def call(kernel, out, *args, specs=None, out_specs=None, scratch=(), mib=32, aliases=None):
    return pl.pallas_call(
        kernel,
        out_shape=out,
        in_specs=specs or [IN_VMEM] * len(args),
        out_specs=out_specs or jax.tree.map(lambda _: IN_VMEM, out),
        scratch_shapes=list(scratch),
        input_output_aliases=aliases or {},
        compiler_params=room(mib),
    )(*args)


def swap(x, axis):
    return lax.all_to_all(x, axis, 0, 0, tiled=True)


def turn(x, axis, by):
    n = lax.axis_size(axis)
    return lax.ppermute(x, axis, [(i, (i + by) % n) for i in range(n)])


def body(activations, cotangent, weight, stats_old, owners, next_acts):
    n_x, n_zh, n_zl, n_feat = (lax.axis_size(a) for a in ("x", "zh", "zl", "feat"))
    rows_dev, columns = weight.shape
    tokens = activations.shape[0]
    owners = owners.T
    shape = jax.ShapeDtypeStruct
    dma = pltpu.SemaphoreType.DMA
    sent = call(
        grad_kernel,
        shape((n_x, SENT, W), BF),
        *[pltpu.with_memory_space_constraint(a, pltpu.HBM) for a in (owners, activations, cotangent, stats_old)],
        specs=[IN_HBM] * 4,
        scratch=[
            pltpu.SMEM(owners.shape, jnp.int32),
            pltpu.VMEM((tokens, rows_dev), BF),
            pltpu.VMEM((tokens, columns), BF),
            pltpu.VMEM((2, W, W), F32),
            pltpu.VMEM((rows_dev, tokens), BF),
            dma((11,)),
        ],
    )
    share = SENT // n_zl
    column = call(sum_kernel, shape((1, SENT, W), BF), swap(sent, "x"))
    column, acts = lax.optimization_barrier((column, next_acts))
    acts_3 = turn(acts, "x", 3)
    tiles = swap(column.reshape(n_zl, share, W), "zl")
    tiles, acts_3 = lax.optimization_barrier((tiles, acts_3))
    part, acts = lax.optimization_barrier((call(sum_kernel, shape((n_zh, share, W), BF), tiles), acts))
    acts_2 = turn(acts, "x", 2)
    tiles, acts_2 = lax.optimization_barrier((swap(part, "zh"), acts_2))
    mine, acts = lax.optimization_barrier((call(sum_kernel, shape((n_zl, share, W), BF), tiles), acts))
    acts_1 = turn(acts, "x", 1)
    full = swap(mine, "zl").reshape(SENT, W)
    acts_1, acts_2, acts_3 = (pltpu.with_memory_space_constraint(a, pltpu.HBM) for a in (acts_1, acts_2, acts_3))
    moved, partial_next = call(
        root_kernel,
        [shape((SENT, W), BF), shape((n_x, W, tokens), BF)],
        full,
        weight,
        pltpu.with_memory_space_constraint(next_acts, pltpu.HBM),
        acts_1,
        acts_2,
        acts_3,
        specs=[IN_VMEM] + [IN_HBM] * 5,
        scratch=[pltpu.VMEM((rows_dev, W), F32), pltpu.VMEM((n_x, tokens, rows_dev), BF), dma((5,))],
        mib=32,
    )
    tiles = swap(partial_next.reshape(n_feat, columns // n_feat, tokens), "feat")
    moved_3, moved_2, moved_1 = turn(moved, "x", 3), turn(moved[:EACH], "x", 2), turn(moved, "x", 1)
    outs = [shape(weight.shape, F32), shape(stats_old.shape, F32)]
    begun = list(call(
        finish_kernel,
        outs,
        owners,
        moved,
        weight,
        stats_old,
        specs=[IN_HBM, IN_VMEM, IN_HBM, IN_HBM],
        out_specs=[IN_HBM, IN_HBM],
        scratch=[
            pltpu.SMEM(owners.shape, jnp.int32),
            pltpu.VMEM((rows_dev, W), F32),
            pltpu.VMEM((2, W, W), F32),
            pltpu.VMEM((rows_dev, W), F32),
            pltpu.VMEM((2, W, W), F32),
            dma((4,)),
            dma((2,)),
        ],
    ))
    begun[0], begun[1], handed = lax.optimization_barrier((*begun, moved_3))
    moved_2 = moved_2, turn(handed[EACH:], "x", 3)
    weight_new, stats_new = call(
        last_kernel,
        outs,
        owners,
        moved_3,
        moved_1,
        *moved_2,
        weight,
        stats_old,
        *begun,
        specs=[IN_HBM] + [IN_VMEM] * 4 + [IN_HBM] * 4,
        out_specs=[IN_HBM, IN_HBM],
        scratch=[
            pltpu.SMEM(owners.shape, jnp.int32),
            pltpu.VMEM((3, rows_dev, W), F32),
            pltpu.VMEM((2, W, W), F32),
            pltpu.VMEM((3, rows_dev, W), F32),
            pltpu.VMEM((W, W), F32),
            dma((6,)),
            dma((4,)),
        ],
        aliases={7: 0, 8: 1},
    )
    summed = jnp.sum(tiles.astype(F32), axis=0).astype(BF)
    each = n_feat // n_x
    pairs = [
        (x * n_feat + to * each + j, to * n_feat + x * each + j)
        for x in range(n_x)
        for to in range(n_x)
        for j in range(each)
    ]
    next_out = lax.ppermute(summed, ("x", "feat"), pairs).T
    return (weight_new, stats_new, next_out)


def solution(mesh):
    torus = Mesh(mesh.devices.reshape(4, 3, 4, mesh.shape["feat"]), ("x", "zh", "zl", "feat"))
    return jax.shard_map(
        body,
        mesh=torus,
        in_specs=(
            P(DP, "feat"),
            P(DP, None),
            P("feat", None),
            P("feat", DP, None, None, None),
            P(),
            P(DP, "feat"),
        ),
        out_specs=(P("feat", None), P("feat", DP, None, None, None), P(DP, "feat")),
        check_vma=False,
    )
```
